32 devices in a mesh: band: 8 (over y, x, core), ga: 4 (over z).
Axes of the slice: x: 2, y: 2, z: 4, core: 2. Of those that a mesh axis runs over, the one named last changes fastest.
Arguments:
- coeffs: float32 [1024, 16384], P('band', 'ga'), may hold values from -90 to 90, as said below
Outputs:
- orthonormal: float32 [1024, 16384], P('band', 'ga')
The draws below stay inside these ranges and needn't reach their ends.
Inputs may be any that keep to these rules, and one draw needn't show every extreme that they name: `coeffs`: bands are linearly independent.
All inputs are finite; a program needn't handle non-finite values.
Results may differ from the reference program's by a relative error of at most 0.00029.
Values sent between devices are 32-bit elements; how exact they have to be, the bound alone decides.
No kernel may reach another device: no remote copies, remote signals or barrier semaphores. Data moves between devices by JAX's collectives and lax.ppermute only.
A program may use at most 128 MiB of HBM per device.

```python
import jax
import jax.numpy as jnp
from jax import lax

NB = 1024
NGT = 16384


def draw_coeffs(key, part):
    key_noise, key_scale, key_common = jax.random.split(key, 3)
    noise = jnp.clip(jax.random.normal(key_noise, (NB, NGT), jnp.float32), -5.0, 5.0)
    common_weight = 0.3
    scales = jnp.exp(jax.random.uniform(key_scale, (NB, 1), jnp.float32, 0.0, 2.302585))
    common = jnp.clip(jax.random.normal(key_common, (1, NGT), jnp.float32), -5.0, 5.0)
    return scales * (noise + 0.6 * jnp.roll(noise, 1, axis=0)) + common_weight * common


def setup_inputs(seed: int = 0) -> dict:
    arg_keys = jax.random.split(jax.random.key(seed), 2)
    coeffs = draw_coeffs(jax.random.fold_in(arg_keys[1], 71), 0)
    return dict(coeffs=coeffs)


def reference(coeffs):
    columns_all = coeffs.shape[1]
    margin = jnp.dot(coeffs.astype(jnp.float32), coeffs.T.astype(jnp.float32), precision=lax.Precision.HIGHEST, preferred_element_type=jnp.float32) / columns_all
    factor = jnp.linalg.cholesky(margin)
    return lax.linalg.triangular_solve(factor, coeffs, left_side=True, lower=True)
```

```python
import functools

import jax
import jax.numpy as jnp
from jax import lax
from jax.experimental import pallas as pl
from jax.experimental.pallas import tpu as pltpu
from jax.sharding import PartitionSpec as P

BLOCK = 128
STRIP = 8
NN = (((1,), (0,)), ((), ()))
NT = (((1,), (1,)), ((), ()))


def halves(x):
    high = x.astype(jnp.bfloat16)
    return high, (x - high.astype(jnp.float32)).astype(jnp.bfloat16)


def left3(x):
    high, low = halves(x)
    return jnp.concatenate([high, low, high], axis=1)


def right3(x):
    high, low = halves(x)
    return jnp.concatenate([high, high, low], axis=0)


def right3t(x):
    high, low = halves(x)
    return jnp.concatenate([high, high, low], axis=1)


def mm(a, b, dims=NN):
    return lax.dot_general(a, b, dims, preferred_element_type=jnp.float32)


def leaf(strips):
    strips = list(strips)
    count = len(strips)
    shape = strips[0].shape
    lane = lax.broadcasted_iota(jnp.int32, shape, 1)
    sub = lax.broadcasted_iota(jnp.int32, shape, 0)
    for s in range(count):
        base = STRIP * s
        rows = [jnp.broadcast_to(strips[s][q : q + 1, :], shape) for q in range(STRIP)]
        piv = [
            [
                jnp.broadcast_to(rows[a][:, base + b : base + b + 1], shape) if b >= a else None
                for b in range(STRIP)
            ]
            for a in range(STRIP)
        ]
        panel = (lane >= base) & (lane < base + STRIP)
        rows = [
            jnp.where(panel, jnp.where(lane == base + q, 1.0, 0.0), rows[q]) for q in range(STRIP)
        ]
        mult = [[None] * STRIP for _ in range(STRIP)]
        done = [None] * STRIP
        gain = [None] * STRIP
        for q in range(STRIP):
            inv = 1.0 / piv[q][q]
            for a in range(q + 1, STRIP):
                mult[a][q] = piv[q][a] * inv
            for a in range(q + 1, STRIP):
                for b in range(a, STRIP):
                    piv[a][b] = piv[a][b] - mult[a][q] * piv[q][b]
                rows[a] = rows[a] - mult[a][q] * rows[q]
            gain[q] = rows[q] * inv
            done[q] = rows[q] * lax.rsqrt(piv[q][q])
        for q in range(STRIP - 1, 0, -1):
            for a in range(q):
                gain[a] = gain[a] - mult[q][a] * gain[q]
        for t in range(s + 1, count):
            terms = [
                jnp.broadcast_to(strips[t][:, base + q : base + q + 1], shape) * gain[q]
                for q in range(STRIP)
            ]
            while len(terms) > 1:
                terms = [terms[i] + terms[i + 1] for i in range(0, len(terms), 2)]
            strips[t] = jnp.where(panel, 0.0, strips[t]) - terms[0]
        new = done[0]
        for q in range(1, STRIP):
            new = jnp.where(sub == q, done[q], new)
        strips[s] = new
    return [jnp.where(lane <= sub + STRIP * s, strips[s], 0.0) for s in range(count)]


def factor_kernel(order, m_ref, x_ref, v_ref, r_ref):
    wide = 2 * BLOCK
    for lo in range(0, order, BLOCK):
        src = m_ref if lo == 0 else x_ref
        hi = lo + BLOCK
        w = jnp.concatenate(leaf([src[lo + s : lo + s + STRIP, lo:hi] for s in range(0, BLOCK, STRIP)]), axis=0)
        w_left, w_rightt = left3(w), right3t(w)
        r_ref[:, lo:hi] = right3(w)
        if hi < order:
            v_ref[: order - hi, :] = left3(mm(left3(src[hi:, lo:hi]), w_rightt, NT))
        for c in range(0, order, wide):
            parts = [(c, c + wide)] if not c <= lo < c + wide else [(c, c + BLOCK), (c + BLOCK, c + wide)]
            for a, b in parts:
                if a == lo:
                    continue
                t = mm(w_left, right3(src[lo:hi, a:b]))
                x_ref[lo:hi, a:b] = t if a < lo else jnp.zeros_like(t)
                r_ref[:, a:b] = right3(t)
        x_ref[lo:hi, lo:hi] = w
        if hi < order:
            for c in range(0, order, wide):
                t = mm(v_ref[: order - hi, :], r_ref[:, c : c + wide])
                if not c <= lo < c + wide:
                    x_ref[hi:, c : c + wide] = src[hi:, c : c + wide] - t
                else:
                    for d in (c, c + BLOCK):
                        part = t[:, d - c : d - c + BLOCK]
                        x_ref[hi:, d : d + BLOCK] = -part if d == lo else src[hi:, d : d + BLOCK] - part


def inverse_factor(margin):
    order = margin.shape[0]
    return pl.pallas_call(
        functools.partial(factor_kernel, order),
        out_shape=jax.ShapeDtypeStruct((order, order), jnp.float32),
        in_specs=[pl.BlockSpec(memory_space=pltpu.VMEM)],
        out_specs=pl.BlockSpec(memory_space=pltpu.VMEM),
        scratch_shapes=[
            pltpu.VMEM((order - BLOCK, 3 * BLOCK), jnp.bfloat16),
            pltpu.VMEM((3 * BLOCK, order), jnp.bfloat16),
        ],
        compiler_params=pltpu.CompilerParams(vmem_limit_bytes=40 * 2**20),
    )(margin)


def local(coeffs):
    band_rows, width = coeffs.shape
    columns_all = width * lax.axis_size("ga")
    gathered = lax.all_gather(coeffs, "band", axis=0, tiled=True)
    partial_value = (
        jnp.dot(
            coeffs, gathered.T, precision=lax.Precision.HIGH, preferred_element_type=jnp.float32
        )
        / columns_all
    )
    summed = lax.psum(partial_value, "ga")
    margin = lax.all_gather(summed, "band", axis=0, tiled=True)
    inverse = inverse_factor(margin)
    own_rows = lax.dynamic_slice_in_dim(inverse, lax.axis_index("band") * band_rows, band_rows, 0)
    return jnp.dot(
        own_rows, gathered, precision=lax.Precision.HIGH, preferred_element_type=jnp.float32
    )


def solution(mesh):
    return jax.shard_map(
        local,
        mesh=mesh,
        in_specs=(P("band", "ga"),),
        out_specs=P("band", "ga"),
        check_vma=False,
    )
```

```python
import functools

import jax
import jax.numpy as jnp
from jax import lax
from jax.experimental import pallas as pl
from jax.experimental.pallas import tpu as pltpu
from jax.sharding import PartitionSpec as P

BLOCK = 128
STRIP = 8
NN = (((1,), (0,)), ((), ()))
NT = (((1,), (1,)), ((), ()))


def halves(x):
    high = x.astype(jnp.bfloat16)
    return high, (x - high.astype(jnp.float32)).astype(jnp.bfloat16)


def left3(x):
    high, low = halves(x)
    return jnp.concatenate([high, low, high], axis=1)


def right3(x):
    high, low = halves(x)
    return jnp.concatenate([high, high, low], axis=0)


def right3t(x):
    high, low = halves(x)
    return jnp.concatenate([high, high, low], axis=1)


def mm(a, b, dims=NN):
    return lax.dot_general(a, b, dims, preferred_element_type=jnp.float32)


def leaf(strips):
    strips = list(strips)
    count = len(strips)
    shape = strips[0].shape
    lane = lax.broadcasted_iota(jnp.int32, shape, 1)
    sub = lax.broadcasted_iota(jnp.int32, shape, 0)
    for s in range(count):
        base = STRIP * s
        rows = [jnp.broadcast_to(strips[s][q : q + 1, :], shape) for q in range(STRIP)]
        piv = [
            [
                jnp.broadcast_to(rows[a][:, base + b : base + b + 1], shape) if b >= a else None
                for b in range(STRIP)
            ]
            for a in range(STRIP)
        ]
        panel = (lane >= base) & (lane < base + STRIP)
        rows = [
            jnp.where(panel, jnp.where(lane == base + q, 1.0, 0.0), rows[q]) for q in range(STRIP)
        ]
        mult = [[None] * STRIP for _ in range(STRIP)]
        done = [None] * STRIP
        gain = [None] * STRIP
        for q in range(STRIP):
            inv = 1.0 / piv[q][q]
            for a in range(q + 1, STRIP):
                mult[a][q] = piv[q][a] * inv
            for a in range(q + 1, STRIP):
                for b in range(a, STRIP):
                    piv[a][b] = piv[a][b] - mult[a][q] * piv[q][b]
                rows[a] = rows[a] - mult[a][q] * rows[q]
            gain[q] = rows[q] * inv
            done[q] = rows[q] * lax.rsqrt(piv[q][q])
        for q in range(STRIP - 1, 0, -1):
            for a in range(q):
                gain[a] = gain[a] - mult[q][a] * gain[q]
        for t in range(s + 1, count):
            terms = [
                jnp.broadcast_to(strips[t][:, base + q : base + q + 1], shape) * gain[q]
                for q in range(STRIP)
            ]
            while len(terms) > 1:
                terms = [terms[i] + terms[i + 1] for i in range(0, len(terms), 2)]
            strips[t] = jnp.where(panel, 0.0, strips[t]) - terms[0]
        new = done[0]
        for q in range(1, STRIP):
            new = jnp.where(sub == q, done[q], new)
        strips[s] = new
    return [jnp.where(lane <= sub + STRIP * s, strips[s], 0.0) for s in range(count)]


def vmem_call(kernel, shapes, scratch, idx, operands, limit=40):
    space = pl.BlockSpec(memory_space=pltpu.VMEM)
    return pl.pallas_call(
        kernel,
        out_shape=shapes,
        in_specs=[pl.BlockSpec(memory_space=pltpu.SMEM)] + [space] * len(operands),
        out_specs=[space] * len(shapes),
        scratch_shapes=scratch,
        compiler_params=pltpu.CompilerParams(vmem_limit_bytes=limit * 2**20),
    )(idx, *operands)


def f32(*shape):
    return jax.ShapeDtypeStruct(shape, jnp.float32)


def cut_kernel(parts, width, idx_ref, x_ref, *outs):
    for d in range(parts):
        start = pl.multiple_of(jnp.bitwise_xor(idx_ref[0], d) * width, width)
        outs[d][...] = x_ref[:, pl.ds(start, width)]


def cut_columns(x, idx, parts):
    width = x.shape[1] // parts
    return vmem_call(
        functools.partial(cut_kernel, parts, width), [f32(x.shape[0], width)] * parts, [], idx, [x]
    )


def join_kernel(parts, width, idx_ref, *refs):
    for d in range(parts):
        start = pl.multiple_of(jnp.bitwise_xor(idx_ref[0], d) * width, width)
        refs[parts][:, pl.ds(start, width)] = refs[d][...]


def join_columns(pieces, idx):
    parts = len(pieces)
    rows, width = pieces[0].shape
    return vmem_call(
        functools.partial(join_kernel, parts, width), [f32(rows, width * parts)], [], idx, pieces
    )[0]


def sum_split_kernel(terms, parts, slot, idx_ref, *refs):
    ins, outs = refs[:terms], refs[terms:]
    rows = outs[0].shape[0]
    for d in range(parts):
        part = pl.ds(pl.multiple_of(jnp.bitwise_xor(idx_ref[slot], d) * rows, 8), rows)
        total = ins[0][part, :]
        for r in ins[1:]:
            total = total + r[part, :]
        outs[d][...] = total


def sum_split(terms, parts, slot, idx):
    rows, width = terms[0].shape
    return vmem_call(
        functools.partial(sum_split_kernel, len(terms), parts, slot),
        [f32(rows // parts, width)] * parts,
        [],
        idx,
        terms,
    )


def lower_blocks(first, last):
    return [(i, j) for i in range(first, last) for j in range(i + 1)]


def gram_kernel(parts, scale, head, order, idx_ref, *refs):
    pieces = refs[:parts]
    outs = refs[parts : parts + 4]
    a_ref, b_ref, flat_ref, flat2_ref = refs[parts + 4 :]
    rows, width = pieces[0].shape
    for d in range(parts):
        at = pl.ds(pl.multiple_of(jnp.bitwise_xor(idx_ref[0], d) * rows, rows), rows)
        high, low = halves(pieces[d][...])
        a_ref[at, 0:width] = high
        a_ref[at, width : 2 * width] = low
        a_ref[at, 2 * width :] = high
        b_ref[at, 0:width] = high
        b_ref[at, width : 2 * width] = high
        b_ref[at, 2 * width :] = low
    place = {}
    for ref, blocks in ((flat_ref, lower_blocks(0, head)), (flat2_ref, lower_blocks(head, order // BLOCK))):
        for n, block in enumerate(blocks):
            half = len(blocks) // 2
            place[block] = (ref, n // half, (n % half) * BLOCK)
    wide = 2 * BLOCK
    for c in range(0, order, wide):
        t = mm(a_ref[c:, :], b_ref[c : c + wide, :], NT) * scale
        for i in range(c // BLOCK, order // BLOCK):
            for j in (c // BLOCK, c // BLOCK + 1):
                if j <= i:
                    ref, half, row = place[i, j]
                    ref[half, row : row + BLOCK, :] = t[
                        i * BLOCK - c : (i + 1) * BLOCK - c, j * BLOCK - c : (j + 1) * BLOCK - c
                    ]
    core = jnp.bitwise_and(idx_ref[0], 1)
    for ref, keep, send in ((flat_ref, outs[0], outs[1]), (flat2_ref, outs[2], outs[3])):
        keep[...] = ref[core]
        send[...] = ref[1 - core]


def gram(pieces, idx, columns_all, head):
    parts = len(pieces)
    rows, width = pieces[0].shape
    order = rows * parts
    r1 = len(lower_blocks(0, head)) * BLOCK // 2
    r2 = len(lower_blocks(head, order // BLOCK)) * BLOCK // 2
    return vmem_call(
        functools.partial(gram_kernel, parts, 1.0 / columns_all, head, order),
        [f32(r1, BLOCK), f32(r1, BLOCK), f32(r2, BLOCK), f32(r2, BLOCK)],
        [
            pltpu.VMEM((order, 3 * width), jnp.bfloat16),
            pltpu.VMEM((order, 3 * width), jnp.bfloat16),
            pltpu.VMEM((2, r1, BLOCK), jnp.float32),
            pltpu.VMEM((2, r2, BLOCK), jnp.float32),
        ],
        idx,
        pieces,
    )


def swap(x, axis, d):
    return lax.ppermute(x, axis, [(i, i ^ d) for i in range(lax.axis_size(axis))])


def sum_everywhere(keep, send, idx):
    chips, depth = lax.axis_size("band") // 2, lax.axis_size("ga")
    got = swap(send, "band", 1)
    pieces = sum_split([keep, got], chips, 1, idx)
    terms = [pieces[0]] + [swap(pieces[d], "band", 2 * d) for d in range(1, chips)]
    if pieces[0].shape[0] % (8 * depth) == 0:
        pieces = sum_split(terms, depth, 2, idx)
        terms = [pieces[0]] + [swap(pieces[d], "ga", d) for d in range(1, depth)]
        own = sum(terms[1:], terms[0])
        mine = jnp.concatenate([own] + [swap(own, "ga", d) for d in range(1, depth)], axis=0)
        cuts = depth
    else:
        mine = lax.psum(sum(terms[1:], terms[0]), "ga")
        cuts = 1
    plane = [mine] + [swap(mine, "band", 2 * d) for d in range(1, chips)]
    return plane + [swap(p, "band", 1) for p in plane], cuts


def gather_flat(pieces, cuts, idx_ref, flat_ref):
    count = len(pieces)
    rows = pieces[0].shape[0] // cuts
    chip_ga = jnp.bitwise_and(idx_ref[0], 1) * (count // 2) + idx_ref[1]
    for e in range(count):
        for z in range(cuts):
            at = jnp.bitwise_xor(chip_ga, e) * cuts
            at = at + (jnp.bitwise_xor(idx_ref[2], z) if cuts > 1 else 0)
            flat_ref[pl.ds(pl.multiple_of(at * rows, 8), rows), :] = pieces[e][z * rows : (z + 1) * rows, :]


def eliminate(x_ref, vl_ref, vr_ref, r_ref, base, lo, order):
    hi = lo + BLOCK
    wide = 2 * BLOCK
    row = slice(lo - base, hi - base)
    w = jnp.concatenate(
        leaf([x_ref[lo - base + s : lo - base + s + STRIP, lo:hi] for s in range(0, BLOCK, STRIP)]),
        axis=0,
    )
    w_left = left3(w)
    r_ref[:, lo:hi] = right3(w)
    rest = order - hi
    if rest:
        v = mm(left3(x_ref[hi - base :, lo:hi]), right3t(w), NT)
        vl_ref[:rest, :] = left3(v)
        vr_ref[:rest, :] = right3t(v)
        for c in range(hi, order, wide):
            d = min(c + wide, order)
            t = mm(vl_ref[c - hi : rest, :], vr_ref[c - hi : d - hi, :], NT)
            x_ref[c - base :, c:d] = x_ref[c - base :, c:d] - t
    for c in range(0, lo, wide):
        d = min(c + wide, lo)
        t = mm(w_left, right3(x_ref[row, c:d]))
        x_ref[row, c:d] = t
        r_ref[:, c:d] = right3(t)
    x_ref[row, lo:hi] = w
    if rest:
        x_ref[row, hi:] = jnp.zeros((BLOCK, rest), jnp.float32)
        for c in range(0, hi, wide):
            d = min(c + wide, hi)
            t = mm(vl_ref[:rest, :], r_ref[:, c:d])
            if d <= lo:
                x_ref[hi - base :, c:d] = x_ref[hi - base :, c:d] - t
            else:
                if c < lo:
                    x_ref[hi - base :, c:lo] = x_ref[hi - base :, c:lo] - t[:, : lo - c]
                x_ref[hi - base :, lo:hi] = -t[:, lo - c :]


def head_kernel(count, cuts, head, idx_ref, *refs):
    pieces, x_ref = refs[:count], refs[count]
    flat_ref, vl_ref, vr_ref, r_ref = refs[count + 1 :]
    gather_flat(pieces, cuts, idx_ref, flat_ref)
    for n, (i, j) in enumerate(lower_blocks(0, head)):
        x_ref[i * BLOCK : (i + 1) * BLOCK, j * BLOCK : (j + 1) * BLOCK] = flat_ref[
            n * BLOCK : (n + 1) * BLOCK, :
        ]
    order = head * BLOCK
    for lo in range(0, order, BLOCK):
        eliminate(x_ref, vl_ref, vr_ref, r_ref, 0, lo, order)


def tail_kernel(count, cuts, head, order, idx_ref, top_ref, *refs):
    pieces, x_ref = refs[:count], refs[count]
    flat_ref, vl_ref, vr_ref, r_ref = refs[count + 1 :]
    base = head * BLOCK
    gather_flat(pieces, cuts, idx_ref, flat_ref)
    for n, (i, j) in enumerate(lower_blocks(head, order // BLOCK)):
        x_ref[i * BLOCK - base : (i + 1) * BLOCK - base, j * BLOCK : (j + 1) * BLOCK] = flat_ref[
            n * BLOCK : (n + 1) * BLOCK, :
        ]
    top_high, top_low = halves(top_ref[...])
    s_high, s_low = halves(x_ref[:, :base])
    v = mm(s_high, top_high, NT) + mm(s_high, top_low, NT) + mm(s_low, top_high, NT)
    v_high, v_low = halves(v)
    x_ref[:, :base] = -(mm(v_high, top_high) + mm(v_high, top_low) + mm(v_low, top_high))
    x_ref[:, base:] = x_ref[:, base:] - (
        mm(v_high, v_high, NT) + mm(v_high, v_low, NT) + mm(v_low, v_high, NT)
    )
    for lo in range(base, order, BLOCK):
        eliminate(x_ref, vl_ref, vr_ref, r_ref, base, lo, order)


def factor_scratch(blocks, rows, order):
    return [
        pltpu.VMEM((len(blocks) * BLOCK, BLOCK), jnp.float32),
        pltpu.VMEM((rows - BLOCK, 3 * BLOCK), jnp.bfloat16),
        pltpu.VMEM((rows - BLOCK, 3 * BLOCK), jnp.bfloat16),
        pltpu.VMEM((3 * BLOCK, order), jnp.bfloat16),
    ]


def head_factor(pieces, cuts, idx, head):
    rows = head * BLOCK
    return vmem_call(
        functools.partial(head_kernel, len(pieces), cuts, head),
        [f32(rows, rows)],
        factor_scratch(lower_blocks(0, head), rows, rows),
        idx,
        pieces,
    )[0]


def tail_factor(top, pieces, cuts, idx, head, order):
    rows = order - head * BLOCK
    return vmem_call(
        functools.partial(tail_kernel, len(pieces), cuts, head, order),
        [f32(rows, order)],
        factor_scratch(lower_blocks(head, order // BLOCK), rows, order),
        idx,
        [top] + list(pieces),
    )[0]


def apply_kernel(parts, head, idx_ref, top_ref, bottom_ref, *refs):
    pieces, outs = refs[:parts], refs[parts : 2 * parts]
    high_ref, low_ref, out_ref = refs[2 * parts :]
    rows = pieces[0].shape[0]
    order = rows * parts
    base = head * BLOCK
    for d in range(parts):
        at = pl.ds(pl.multiple_of(jnp.bitwise_xor(idx_ref[0], d) * rows, rows), rows)
        high_ref[at, :], low_ref[at, :] = halves(pieces[d][...])
    wide = 2 * BLOCK
    for r in range(0, order, wide):
        k = r + wide
        x = top_ref[r:k, :k] if k <= base else bottom_ref[r - base : k - base, :k]
        x_high, x_low = halves(x)
        out_ref[r:k, :] = mm(x_high, high_ref[:k, :]) + mm(x_high, low_ref[:k, :]) + mm(x_low, high_ref[:k, :])
    for d in range(parts):
        at = pl.ds(pl.multiple_of(jnp.bitwise_xor(idx_ref[0], d) * rows, rows), rows)
        outs[d][...] = out_ref[at, :]


def apply(top, bottom, pieces, idx, head):
    parts = len(pieces)
    rows, width = pieces[0].shape
    order = rows * parts
    return vmem_call(
        functools.partial(apply_kernel, parts, head),
        [f32(rows, width)] * parts,
        [
            pltpu.VMEM((order, width), jnp.bfloat16),
            pltpu.VMEM((order, width), jnp.bfloat16),
            pltpu.VMEM((order, width), jnp.float32),
        ],
        idx,
        [top, bottom] + list(pieces),
    )


def local(coeffs):
    band_rows, width = coeffs.shape
    parts = lax.axis_size("band")
    order = band_rows * parts
    columns_all = width * lax.axis_size("ga")
    head = order // BLOCK // 2
    band = lax.axis_index("band")
    idx = jnp.stack([band, band // 2, lax.axis_index("ga")]).astype(jnp.int32)
    pieces = cut_columns(coeffs, idx, parts)
    pieces = [pieces[0]] + [swap(pieces[d], "band", d) for d in range(1, parts)]
    keep1, send1, keep2, send2 = gram(pieces, idx, columns_all, head)
    flat1, cuts1 = sum_everywhere(keep1, send1, idx)
    flat2, cuts2 = sum_everywhere(keep2, send2, idx)
    top = head_factor(flat1, cuts1, idx, head)
    bottom = tail_factor(top, flat2, cuts2, idx, head, order)
    result = apply(top, bottom, pieces, idx, head)
    result = [result[0]] + [swap(result[d], "band", d) for d in range(1, parts)]
    return join_columns(result, idx)


def solution(mesh):
    return jax.shard_map(
        local,
        mesh=mesh,
        in_specs=(P("band", "ga"),),
        out_specs=P("band", "ga"),
        check_vma=False,
    )
```

```python
import functools

import jax
import jax.numpy as jnp
from jax import lax
from jax.experimental import pallas as pl
from jax.experimental.pallas import tpu as pltpu
from jax.sharding import PartitionSpec as P

BLOCK = 128
STRIP = 8
NN = (((1,), (0,)), ((), ()))
NT = (((1,), (1,)), ((), ()))


def halves(x):
    high = x.astype(jnp.bfloat16)
    return high, (x - high.astype(jnp.float32)).astype(jnp.bfloat16)


def left3(x):
    high, low = halves(x)
    return jnp.concatenate([high, low, high], axis=1)


def right3(x):
    high, low = halves(x)
    return jnp.concatenate([high, high, low], axis=0)


def right3t(x):
    high, low = halves(x)
    return jnp.concatenate([high, high, low], axis=1)


def mm(a, b, dims=NN):
    return lax.dot_general(a, b, dims, preferred_element_type=jnp.float32)


NEAR = 2


def leaf(strips, row_ref, col_ref):
    strips = list(strips)
    count = len(strips)
    shape = strips[0].shape
    lane = lax.broadcasted_iota(jnp.int32, shape, 1)
    sub = lax.broadcasted_iota(jnp.int32, shape, 0)
    each = range(STRIP)

    def column(x, c):
        return jnp.broadcast_to(x[:, c : c + 1], shape)

    def repeated(ref, r):
        return jnp.broadcast_to(ref[r : r + 1, :], shape)

    for s in range(count):
        base = STRIP * s
        row_ref[base : base + STRIP, :] = strips[s]
        for b in each:
            at = (base + b) * STRIP
            col_ref[at : at + STRIP, :] = column(strips[s], base + b)
        rows = [repeated(row_ref, base + q) for q in each]
        piv = [
            [repeated(col_ref, (base + b) * STRIP + a) if b >= a else None for b in each] for a in each
        ]
        panel = (lane >= base) & (lane < base + STRIP)
        rows = [jnp.where(panel, jnp.where(lane == base + q, 1.0, 0.0), rows[q]) for q in each]
        mult = [[None] * STRIP for _ in each]
        done = [None] * STRIP
        gain = [None] * STRIP
        for q in each:
            root = lax.rsqrt(piv[q][q])
            inv = root * root
            for a in range(q + 1, STRIP):
                mult[a][q] = piv[q][a] * inv
            for a in range(q + 1, STRIP):
                for b in range(a, STRIP):
                    piv[a][b] = piv[a][b] - mult[a][q] * piv[q][b]
                rows[a] = rows[a] - mult[a][q] * rows[q]
            gain[q] = rows[q] * inv
            done[q] = rows[q] * root
        for q in range(STRIP - 1, 0, -1):
            for a in range(q):
                gain[a] = gain[a] - mult[q][a] * gain[q]
        far = s + 1 + NEAR
        for t in range(s + 1, min(far, count)):
            terms = [column(strips[t], base + q) * gain[q] for q in each]
            while len(terms) > 1:
                terms = [terms[i] + terms[i + 1] for i in range(0, len(terms), 2)]
            strips[t] = jnp.where(panel, 0.0, strips[t]) - terms[0]
        if far < count:
            g = gain[0]
            for q in range(1, STRIP):
                g = jnp.where(sub == q, gain[q], g)
            below = STRIP * (count - s - 1)

            def padded(x):
                parts = [x]
                if base:
                    parts = [jnp.zeros((base, BLOCK), x.dtype)] + parts
                if below:
                    parts = parts + [jnp.zeros((below, BLOCK), x.dtype)]
                return jnp.concatenate(parts, axis=0)

            g_high, g_low = [padded(x) for x in halves(g)]
            s_high, s_low = halves(jnp.concatenate(strips[far:], axis=0))
            t = mm(
                jnp.concatenate([s_high, s_low], axis=1), jnp.concatenate([g_high, g_high], axis=0)
            ) + mm(s_high, g_low)
            for i in range(far, count):
                at = STRIP * (i - far)
                strips[i] = jnp.where(panel, 0.0, strips[i]) - t[at : at + STRIP, :]
        new = done[0]
        for q in range(1, STRIP):
            new = jnp.where(sub == q, done[q], new)
        strips[s] = new
    return [jnp.where(lane <= sub + STRIP * s, strips[s], 0.0) for s in range(count)]


def vmem_call(kernel, shapes, scratch, idx, operands, cost=1):
    space = pl.BlockSpec(memory_space=pltpu.VMEM)
    return pl.pallas_call(
        kernel,
        out_shape=shapes,
        in_specs=[pl.BlockSpec(memory_space=pltpu.SMEM)] + [space] * len(operands),
        out_specs=[space] * len(shapes),
        scratch_shapes=scratch,
        compiler_params=pltpu.CompilerParams(vmem_limit_bytes=40 * 2**20),
        cost_estimate=pl.CostEstimate(
            flops=cost * 1_000_000_000, bytes_accessed=0, transcendentals=0
        ),
    )(idx, *operands)


def f32(*shape):
    return jax.ShapeDtypeStruct(shape, jnp.float32)


def cut_kernel(parts, width, idx_ref, x_ref, *outs):
    for d in range(parts):
        start = pl.multiple_of(jnp.bitwise_xor(idx_ref[0], d) * width, width)
        outs[d][...] = x_ref[:, pl.ds(start, width)]


def cut_columns(x, idx, parts):
    width = x.shape[1] // parts
    return vmem_call(
        functools.partial(cut_kernel, parts, width), [f32(x.shape[0], width)] * parts, [], idx, [x]
    )


def join_kernel(parts, width, idx_ref, *refs):
    for d in range(parts):
        start = pl.multiple_of(jnp.bitwise_xor(idx_ref[0], d) * width, width)
        refs[parts][:, pl.ds(start, width)] = refs[d][...]


def join_columns(pieces, idx):
    parts = len(pieces)
    rows, width = pieces[0].shape
    return vmem_call(
        functools.partial(join_kernel, parts, width), [f32(rows, width * parts)], [], idx, pieces
    )[0]


def sum_split_kernel(terms, parts, slot, idx_ref, *refs):
    ins, outs = refs[:terms], refs[terms:]
    rows = outs[0].shape[0]
    for d in range(parts):
        part = pl.ds(pl.multiple_of(jnp.bitwise_xor(idx_ref[slot], d) * rows, 8), rows)
        total = ins[0][part, :]
        for r in ins[1:]:
            total = total + r[part, :]
        outs[d][...] = total


def sum_split(terms, parts, slot, idx):
    rows, width = terms[0].shape
    return vmem_call(
        functools.partial(sum_split_kernel, len(terms), parts, slot),
        [f32(rows // parts, width)] * parts,
        [],
        idx,
        terms,
    )


def lower_blocks(first, last):
    return [(i, j) for i in range(first, last) for j in range(i + 1)]


def gram_kernel(parts, scale, head, order, idx_ref, *refs):
    pieces = refs[:parts]
    outs = refs[parts : parts + 4]
    a_ref, b_ref, flat_ref, flat2_ref = refs[parts + 4 :]
    rows, width = pieces[0].shape
    for d in range(parts):
        at = pl.ds(pl.multiple_of(jnp.bitwise_xor(idx_ref[0], d) * rows, rows), rows)
        high, low = halves(pieces[d][...])
        a_ref[at, 0:width] = high
        a_ref[at, width : 2 * width] = low
        a_ref[at, 2 * width :] = high
        b_ref[at, 0:width] = high
        b_ref[at, width : 2 * width] = high
        b_ref[at, 2 * width :] = low
    place = {}
    for ref, blocks in ((flat_ref, lower_blocks(0, head)), (flat2_ref, lower_blocks(head, order // BLOCK))):
        for n, block in enumerate(blocks):
            half = len(blocks) // 2
            place[block] = (ref, n // half, (n % half) * BLOCK)
    wide = 2 * BLOCK
    for c in range(0, order, wide):
        t = mm(a_ref[c:, :], b_ref[c : c + wide, :], NT) * scale
        for i in range(c // BLOCK, order // BLOCK):
            for j in (c // BLOCK, c // BLOCK + 1):
                if j <= i:
                    ref, half, row = place[i, j]
                    ref[half, row : row + BLOCK, :] = t[
                        i * BLOCK - c : (i + 1) * BLOCK - c, j * BLOCK - c : (j + 1) * BLOCK - c
                    ]
    core = jnp.bitwise_and(idx_ref[0], 1)
    for ref, keep, send in ((flat_ref, outs[0], outs[1]), (flat2_ref, outs[2], outs[3])):
        keep[...] = ref[core]
        send[...] = ref[1 - core]


def gram(pieces, idx, columns_all, head):
    parts = len(pieces)
    rows, width = pieces[0].shape
    order = rows * parts
    r1 = len(lower_blocks(0, head)) * BLOCK // 2
    r2 = len(lower_blocks(head, order // BLOCK)) * BLOCK // 2
    return vmem_call(
        functools.partial(gram_kernel, parts, 1.0 / columns_all, head, order),
        [f32(r1, BLOCK), f32(r1, BLOCK), f32(r2, BLOCK), f32(r2, BLOCK)],
        [
            pltpu.VMEM((order, 3 * width), jnp.bfloat16),
            pltpu.VMEM((order, 3 * width), jnp.bfloat16),
            pltpu.VMEM((2, r1, BLOCK), jnp.float32),
            pltpu.VMEM((2, r2, BLOCK), jnp.float32),
        ],
        idx,
        pieces,
    )


def swap(x, axis, d):
    return lax.ppermute(x, axis, [(i, i ^ d) for i in range(lax.axis_size(axis))])


def after(x, y):
    return lax.optimization_barrier((x, y))[0]


def sum_all(terms):
    return sum(terms[1:], terms[0])


def sum_first(keep, send, idx):
    chips, depth = lax.axis_size("band") // 2, lax.axis_size("ga")
    pieces = sum_split([keep, swap(send, "band", 1)], chips, 1, idx)
    part = sum_all([pieces[0]] + [swap(pieces[d], "band", 2 * d) for d in range(1, chips)])
    if depth <= 4:
        total = sum_all([part] + [swap(part, "ga", d) for d in range(1, depth)])
    else:
        total = lax.psum(part, "ga")
    return lax.all_gather(total, "band", axis=0, tiled=True), (pieces[0], part, total)


def sum_second(keep, send, marks, idx):
    chips, depth = lax.axis_size("band") // 2, lax.axis_size("ga")
    pieces = sum_split([keep, swap(after(send, marks[0]), "band", 1)], chips, 1, idx)
    pieces = [pieces[0]] + [after(pieces[d], marks[1]) for d in range(1, chips)]
    plane = [pieces[0]] + [swap(pieces[d], "band", 2 * d) for d in range(1, chips)]
    if depth > 4:
        return lax.psum(sum_all(plane), "ga")
    pieces = sum_split(plane, depth, 2, idx)
    pieces = [pieces[0]] + [after(pieces[d], marks[2]) for d in range(1, depth)]
    return sum_all([pieces[0]] + [swap(pieces[d], "ga", d) for d in range(1, depth)])


def gather_ga(own, mark):
    depth = lax.axis_size("ga")
    if depth > 4:
        return own
    own = after(own, mark)
    return jnp.concatenate([own] + [swap(own, "ga", d) for d in range(1, depth)], axis=0)


def gather_chips(own, mark):
    parts = lax.axis_size("band")
    own = after(own, mark)
    groups = [list(range(core, parts, 2)) for core in range(2)]
    copies = jnp.broadcast_to(own, (parts // 2, *own.shape))
    got = lax.all_to_all(copies, "band", 0, 0, axis_index_groups=groups)
    return got.reshape(-1, own.shape[1])


def place_bands(first_ref, parts, flat_ref):
    rows = first_ref.shape[0] // parts
    for band in range(parts):
        at = ((band % 2) * (parts // 2) + band // 2) * rows
        flat_ref[at : at + rows, :] = first_ref[band * rows : (band + 1) * rows, :]


def place_offsets(halves_, chips, cuts, idx_ref, flat_ref):
    rows = halves_[0].shape[0] // (chips * cuts)
    for c, ref in enumerate(halves_):
        core = jnp.bitwise_xor(jnp.bitwise_and(idx_ref[0], 1), c)
        for chip in range(chips):
            for z in range(cuts):
                at = (core * chips + chip) * cuts
                at = at + (jnp.bitwise_xor(idx_ref[2], z) if cuts > 1 else 0)
                start = (chip * cuts + z) * rows
                flat_ref[pl.ds(pl.multiple_of(at * rows, 8), rows), :] = ref[start : start + rows, :]


def eliminate(x_ref, vl_ref, vr_ref, r_ref, row_ref, col_ref, base, lo, order):
    hi = lo + BLOCK
    wide = 2 * BLOCK
    row = slice(lo - base, hi - base)
    w = jnp.concatenate(
        leaf(
            [x_ref[lo - base + s : lo - base + s + STRIP, lo:hi] for s in range(0, BLOCK, STRIP)],
            row_ref,
            col_ref,
        ),
        axis=0,
    )
    w_left = left3(w)
    r_ref[:, lo:hi] = right3(w)
    rest = order - hi
    if rest:
        v = mm(left3(x_ref[hi - base :, lo:hi]), right3t(w), NT)
        vl_ref[:rest, :] = left3(v)
        vr_ref[:rest, :] = right3t(v)
        for c in range(hi, order, wide):
            d = min(c + wide, order)
            t = mm(vl_ref[c - hi : rest, :], vr_ref[c - hi : d - hi, :], NT)
            x_ref[c - base :, c:d] = x_ref[c - base :, c:d] - t
    for c in range(0, lo, wide):
        d = min(c + wide, lo)
        t = mm(w_left, right3(x_ref[row, c:d]))
        x_ref[row, c:d] = t
        r_ref[:, c:d] = right3(t)
    x_ref[row, lo:hi] = w
    if rest:
        x_ref[row, hi:] = jnp.zeros((BLOCK, rest), jnp.float32)
        for c in range(0, hi, wide):
            d = min(c + wide, hi)
            t = mm(vl_ref[:rest, :], r_ref[:, c:d])
            if d <= lo:
                x_ref[hi - base :, c:d] = x_ref[hi - base :, c:d] - t
            else:
                if c < lo:
                    x_ref[hi - base :, c:lo] = x_ref[hi - base :, c:lo] - t[:, : lo - c]
                x_ref[hi - base :, lo:hi] = -t[:, lo - c :]


def head_kernel(parts, head, idx_ref, first_ref, x_ref, flat_ref, *work):
    place_bands(first_ref, parts, flat_ref)
    for n, (i, j) in enumerate(lower_blocks(0, head)):
        x_ref[i * BLOCK : (i + 1) * BLOCK, j * BLOCK : (j + 1) * BLOCK] = flat_ref[
            n * BLOCK : (n + 1) * BLOCK, :
        ]
    order = head * BLOCK
    for lo in range(0, order // 2, BLOCK):
        eliminate(x_ref, *work, 0, lo, order)


def neck_kernel(head, idx_ref, in_ref, x_ref, *work):
    x_ref[...] = in_ref[...]
    order = head * BLOCK
    for lo in range(order // 2, order, BLOCK):
        eliminate(x_ref, *work, 0, lo, order)


def tail_kernel(chips, cuts, head, order, idx_ref, top_ref, near_ref, far_ref, x_ref, flat_ref, *work):
    base = head * BLOCK
    place_offsets([near_ref, far_ref], chips, cuts, idx_ref, flat_ref)
    for n, (i, j) in enumerate(lower_blocks(head, order // BLOCK)):
        x_ref[i * BLOCK - base : (i + 1) * BLOCK - base, j * BLOCK : (j + 1) * BLOCK] = flat_ref[
            n * BLOCK : (n + 1) * BLOCK, :
        ]
    top_high, top_low = halves(top_ref[...])
    s_high, s_low = halves(x_ref[:, :base])
    v = mm(s_high, top_high, NT) + mm(s_high, top_low, NT) + mm(s_low, top_high, NT)
    v_high, v_low = halves(v)
    x_ref[:, :base] = -(mm(v_high, top_high) + mm(v_high, top_low) + mm(v_low, top_high))
    x_ref[:, base:] = x_ref[:, base:] - (
        mm(v_high, v_high, NT) + mm(v_high, v_low, NT) + mm(v_low, v_high, NT)
    )
    for lo in range(base, order, BLOCK):
        eliminate(x_ref, *work, base, lo, order)


def factor_scratch(blocks, rows, order):
    return [
        pltpu.VMEM((len(blocks) * BLOCK, BLOCK), jnp.float32),
        pltpu.VMEM((rows - BLOCK, 3 * BLOCK), jnp.bfloat16),
        pltpu.VMEM((rows - BLOCK, 3 * BLOCK), jnp.bfloat16),
        pltpu.VMEM((3 * BLOCK, order), jnp.bfloat16),
        pltpu.VMEM((BLOCK, BLOCK), jnp.float32),
        pltpu.VMEM((BLOCK * STRIP, BLOCK), jnp.float32),
    ]


def head_factor(first, parts, idx, head):
    rows = head * BLOCK
    return vmem_call(
        functools.partial(head_kernel, parts, head),
        [f32(rows, rows)],
        factor_scratch(lower_blocks(0, head), rows, rows),
        idx,
        [first],
        cost=60,
    )[0]


def neck_factor(started, idx, head):
    rows = head * BLOCK
    return vmem_call(
        functools.partial(neck_kernel, head),
        [f32(rows, rows)],
        factor_scratch([], rows, rows)[1:],
        idx,
        [started],
        cost=60,
    )[0]


def tail_factor(top, second, chips, cuts, idx, head, order):
    rows = order - head * BLOCK
    return vmem_call(
        functools.partial(tail_kernel, chips, cuts, head, order),
        [f32(rows, order)],
        factor_scratch(lower_blocks(head, order // BLOCK), rows, order),
        idx,
        [top, *second],
        cost=25,
    )[0]


def apply_kernel(parts, head, idx_ref, top_ref, bottom_ref, *refs):
    pieces, outs = refs[:parts], refs[parts : 2 * parts]
    high_ref, low_ref, out_ref = refs[2 * parts :]
    rows = pieces[0].shape[0]
    order = rows * parts
    base = head * BLOCK
    for d in range(parts):
        at = pl.ds(pl.multiple_of(jnp.bitwise_xor(idx_ref[0], d) * rows, rows), rows)
        high_ref[at, :], low_ref[at, :] = halves(pieces[d][...])
    wide = 2 * BLOCK
    for r in range(0, order, wide):
        k = r + wide
        x = top_ref[r:k, :k] if k <= base else bottom_ref[r - base : k - base, :k]
        x_high, x_low = halves(x)
        out_ref[r:k, :] = mm(x_high, high_ref[:k, :]) + mm(x_high, low_ref[:k, :]) + mm(x_low, high_ref[:k, :])
    for d in range(parts):
        at = pl.ds(pl.multiple_of(jnp.bitwise_xor(idx_ref[0], d) * rows, rows), rows)
        outs[d][...] = out_ref[at, :]


def apply(top, bottom, pieces, idx, head):
    parts = len(pieces)
    rows, width = pieces[0].shape
    order = rows * parts
    return vmem_call(
        functools.partial(apply_kernel, parts, head),
        [f32(rows, width)] * parts,
        [
            pltpu.VMEM((order, width), jnp.bfloat16),
            pltpu.VMEM((order, width), jnp.bfloat16),
            pltpu.VMEM((order, width), jnp.float32),
        ],
        idx,
        [top, bottom] + list(pieces),
    )


def local(coeffs):
    band_rows, width = coeffs.shape
    parts = lax.axis_size("band")
    order = band_rows * parts
    columns_all = width * lax.axis_size("ga")
    head = order // BLOCK // 2
    band = lax.axis_index("band")
    idx = jnp.stack([band, band // 2, lax.axis_index("ga")]).astype(jnp.int32)
    pieces = cut_columns(coeffs, idx, parts)
    pieces = [pieces[0]] + [swap(pieces[d], "band", d) for d in range(1, parts)]
    keep1, send1, keep2, send2 = gram(pieces, idx, columns_all, head)
    cuts = lax.axis_size("ga") if lax.axis_size("ga") <= 4 else 1
    first, marks = sum_first(keep1, send1, idx)
    second = sum_second(keep2, send2, marks, idx)
    second = gather_ga(second, first)
    started = head_factor(first, parts, idx, head)
    second = gather_chips(second, started)
    top = neck_factor(started, idx, head)
    second = after(second, top)
    bottom = tail_factor(
        top, (second, swap(second, "band", 1)), parts // 2, cuts, idx, head, order
    )
    result = apply(top, bottom, pieces, idx, head)
    result = [result[0]] + [swap(result[d], "band", d) for d in range(1, parts)]
    return join_columns(result, idx)


def solution(mesh):
    return jax.shard_map(
        local,
        mesh=mesh,
        in_specs=(P("band", "ga"),),
        out_specs=P("band", "ga"),
        check_vma=False,
    )
```

```python
import functools

import jax
import jax.numpy as jnp
from jax import lax
from jax.experimental import pallas as pl
from jax.experimental.pallas import tpu as pltpu
from jax.sharding import PartitionSpec as P

BLOCK = 128
STRIP = 8
NN = (((1,), (0,)), ((), ()))
NT = (((1,), (1,)), ((), ()))


def halves(x):
    high = x.astype(jnp.bfloat16)
    return high, (x - high.astype(jnp.float32)).astype(jnp.bfloat16)


def left3(x):
    high, low = halves(x)
    return jnp.concatenate([high, low, high], axis=1)


def right3(x):
    high, low = halves(x)
    return jnp.concatenate([high, high, low], axis=0)


def right3t(x):
    high, low = halves(x)
    return jnp.concatenate([high, high, low], axis=1)


def mm(a, b, dims=NN):
    return lax.dot_general(a, b, dims, preferred_element_type=jnp.float32)


NEAR = 2


def leaf(strips, row_ref, col_ref, pending):
    share = -(-len(pending) // (BLOCK // STRIP - 4))
    strips = list(strips)
    count = len(strips)
    shape = strips[0].shape
    lane = lax.broadcasted_iota(jnp.int32, shape, 1)
    sub = lax.broadcasted_iota(jnp.int32, shape, 0)
    each = range(STRIP)

    def column(x, c):
        return jnp.broadcast_to(x[:, c : c + 1], shape)

    def repeated(ref, r):
        return jnp.broadcast_to(ref[r : r + 1, :], shape)

    for s in range(count):
        base = STRIP * s
        row_ref[base : base + STRIP, :] = strips[s]
        for b in each:
            at = (base + b) * STRIP
            col_ref[at : at + STRIP, :] = column(strips[s], base + b)
        rows = [repeated(row_ref, base + q) for q in each]
        piv = [
            [repeated(col_ref, (base + b) * STRIP + a) if b >= a else None for b in each] for a in each
        ]
        panel = (lane >= base) & (lane < base + STRIP)
        rows = [jnp.where(panel, jnp.where(lane == base + q, 1.0, 0.0), rows[q]) for q in each]
        mult = [[None] * STRIP for _ in each]
        done = [None] * STRIP
        gain = [None] * STRIP
        for q in each:
            root = lax.rsqrt(piv[q][q])
            inv = root * root
            for a in range(q + 1, STRIP):
                mult[a][q] = piv[q][a] * inv
            for a in range(q + 1, STRIP):
                for b in range(a, STRIP):
                    piv[a][b] = piv[a][b] - mult[a][q] * piv[q][b]
                rows[a] = rows[a] - mult[a][q] * rows[q]
            gain[q] = rows[q] * inv
            done[q] = rows[q] * root
        for q in range(STRIP - 1, 0, -1):
            for a in range(q):
                gain[a] = gain[a] - mult[q][a] * gain[q]
        far = s + 1 + NEAR
        for t in range(s + 1, min(far, count)):
            terms = [column(strips[t], base + q) * gain[q] for q in each]
            while len(terms) > 1:
                terms = [terms[i] + terms[i + 1] for i in range(0, len(terms), 2)]
            strips[t] = jnp.where(panel, 0.0, strips[t]) - terms[0]
        if far < count:
            g = gain[0]
            for q in range(1, STRIP):
                g = jnp.where(sub == q, gain[q], g)
            below = STRIP * (count - s - 1)

            def padded(x):
                parts = [x]
                if base:
                    parts = [jnp.zeros((base, BLOCK), x.dtype)] + parts
                if below:
                    parts = parts + [jnp.zeros((below, BLOCK), x.dtype)]
                return jnp.concatenate(parts, axis=0)

            g_high, g_low = [padded(x) for x in halves(g)]
            s_high, s_low = halves(jnp.concatenate(strips[far:], axis=0))
            t = mm(
                jnp.concatenate([s_high, s_low], axis=1), jnp.concatenate([g_high, g_high], axis=0)
            ) + mm(s_high, g_low)
            for i in range(far, count):
                at = STRIP * (i - far)
                strips[i] = jnp.where(panel, 0.0, strips[i]) - t[at : at + STRIP, :]
        new = done[0]
        for q in range(1, STRIP):
            new = jnp.where(sub == q, done[q], new)
        strips[s] = new
        for _ in range(min(share, len(pending))):
            pending.pop(0)()
    return [jnp.where(lane <= sub + STRIP * s, strips[s], 0.0) for s in range(count)]


def vmem_call(kernel, shapes, scratch, idx, operands, cost=1, vmem=12):
    space = pl.BlockSpec(memory_space=pltpu.VMEM)
    return pl.pallas_call(
        kernel,
        out_shape=shapes,
        in_specs=[pl.BlockSpec(memory_space=pltpu.SMEM)] + [space] * len(operands),
        out_specs=[space] * len(shapes),
        scratch_shapes=scratch,
        compiler_params=pltpu.CompilerParams(vmem_limit_bytes=vmem * 2**20),
        cost_estimate=pl.CostEstimate(
            flops=cost * 1_000_000_000, bytes_accessed=0, transcendentals=0
        ),
    )(idx, *operands)


def f32(*shape):
    return jax.ShapeDtypeStruct(shape, jnp.float32)


def cut_columns(x, band, parts):
    width = x.shape[1] // parts
    return [lax.dynamic_slice_in_dim(x, (band ^ d) * width, width, 1) for d in range(parts)]


def join_kernel(parts, width, idx_ref, *refs):
    for d in range(parts):
        start = pl.multiple_of(jnp.bitwise_xor(idx_ref[0], d) * width, width)
        refs[parts][:, pl.ds(start, width)] = refs[d][...]


def join_columns(pieces, idx):
    parts = len(pieces)
    rows, width = pieces[0].shape
    return vmem_call(
        functools.partial(join_kernel, parts, width), [f32(rows, width * parts)], [], idx, pieces, vmem=8
    )[0]


def sum_split_kernel(terms, sections, parts, slot, idx_ref, *refs):
    ins, outs = refs[:terms], list(refs[terms:])
    first = 0
    for length in sections:
        rows = length // parts
        for d in range(parts):
            start = first + jnp.bitwise_xor(idx_ref[slot], d) * rows
            part = pl.ds(pl.multiple_of(start, 8), rows)
            total = ins[0][part, :]
            for r in ins[1:]:
                total = total + r[part, :]
            outs.pop(0)[...] = total
        first += length


def sum_split(terms, sections, parts, slot, idx):
    width = terms[0].shape[1]
    cut = vmem_call(
        functools.partial(sum_split_kernel, len(terms), sections, parts, slot),
        [f32(length // parts, width) for length in sections for _ in range(parts)],
        [],
        idx,
        terms,
    )
    return [cut[n * parts : (n + 1) * parts] for n in range(len(sections))]


def lower_blocks(first, last):
    return [(i, j) for i in range(first, last) for j in range(i + 1)]


def mm3(a_high, a_low, b_high, b_low, dims=NN):
    return mm(a_high, b_high, dims) + mm(a_high, b_low, dims) + mm(a_low, b_high, dims)


def gram_kernel(parts, scale, head, order, idx_ref, *refs):
    pieces = refs[:parts]
    keep_ref, send_ref, high_ref, low_ref, flat_ref = refs[parts:]
    rows = pieces[0].shape[0]
    for d in range(parts):
        at = pl.ds(pl.multiple_of(jnp.bitwise_xor(idx_ref[0], d) * rows, rows), rows)
        high_ref[at, :], low_ref[at, :] = halves(pieces[d][...])
    place = {}
    first = 0
    for blocks in (lower_blocks(0, head), lower_blocks(head, order // BLOCK)):
        half = len(blocks) // 2
        for n, block in enumerate(blocks):
            place[block] = (n // half, first + n % half * BLOCK)
        first += half * BLOCK
    wide = 2 * BLOCK
    for c in range(0, order, wide):
        t = scale * mm3(
            high_ref[c:, :], low_ref[c:, :], high_ref[c : c + wide, :], low_ref[c : c + wide, :], NT
        )
        for i in range(c // BLOCK, order // BLOCK):
            for j in (c // BLOCK, c // BLOCK + 1):
                if j <= i:
                    half, row = place[i, j]
                    flat_ref[half, row : row + BLOCK, :] = t[
                        i * BLOCK - c : (i + 1) * BLOCK - c, j * BLOCK - c : (j + 1) * BLOCK - c
                    ]
    core = jnp.bitwise_and(idx_ref[0], 1)
    keep_ref[...] = flat_ref[core]
    send_ref[...] = flat_ref[1 - core]


def gram(pieces, idx, columns_all, head):
    parts = len(pieces)
    rows, width = pieces[0].shape
    order = rows * parts
    length = len(lower_blocks(0, order // BLOCK)) * BLOCK // 2
    term = jax.ShapeDtypeStruct((order, width), jnp.bfloat16)
    return vmem_call(
        functools.partial(gram_kernel, parts, 1.0 / columns_all, head, order),
        [f32(length, BLOCK), f32(length, BLOCK), term, term],
        [pltpu.VMEM((2, length, BLOCK), jnp.float32)],
        idx,
        pieces,
        vmem=20,
    )


def swap(x, axis, d):
    return lax.ppermute(x, axis, [(i, i ^ d) for i in range(lax.axis_size(axis))])


def sum_all(terms):
    return sum(terms[1:], terms[0])


def sum_band(keep, send, head, order, idx):
    chips = lax.axis_size("band") // 2
    sections = [
        len(blocks) * BLOCK // 2 for blocks in (lower_blocks(0, head), lower_blocks(head, order // BLOCK))
    ]
    return sum_split([keep, swap(send, "band", 1)], sections, chips, 1, idx)


def sum_chips(pieces):
    return [pieces[0]] + [swap(pieces[d], "band", 2 * d) for d in range(1, len(pieces))]


def sum_first(terms):
    depth = lax.axis_size("ga")
    part = sum_all(terms)
    if depth <= 4:
        total = sum_all([part] + [swap(part, "ga", d) for d in range(1, depth)])
    else:
        total = lax.psum(part, "ga")
    return lax.all_gather(total, "band", axis=0, tiled=True)


def sum_second(terms, idx):
    depth = lax.axis_size("ga")
    if depth > 4:
        return lax.psum(sum_all(terms), "ga")
    pieces = sum_split(terms, [terms[0].shape[0]], depth, 2, idx)[0]
    return sum_all([pieces[0]] + [swap(pieces[d], "ga", d) for d in range(1, depth)])


def gather_ga(own):
    depth = lax.axis_size("ga")
    if depth > 4:
        return own
    return jnp.concatenate([own] + [swap(own, "ga", d) for d in range(1, depth)], axis=0)


def gather_chips(own):
    parts = lax.axis_size("band")
    groups = [list(range(core, parts, 2)) for core in range(2)]
    copies = jnp.broadcast_to(own, (parts // 2, *own.shape))
    got = lax.all_to_all(copies, "band", 0, 0, axis_index_groups=groups)
    return got.reshape(-1, own.shape[1])


def place_bands(first_ref, parts, flat_ref):
    rows = first_ref.shape[0] // parts
    for band in range(parts):
        at = ((band % 2) * (parts // 2) + band // 2) * rows
        flat_ref[at : at + rows, :] = first_ref[band * rows : (band + 1) * rows, :]


def place_offsets(halves_, chips, cuts, idx_ref, flat_ref):
    rows = halves_[0].shape[0] // (chips * cuts)
    for c, ref in enumerate(halves_):
        core = jnp.bitwise_xor(jnp.bitwise_and(idx_ref[0], 1), c)
        for chip in range(chips):
            for z in range(cuts):
                at = (core * chips + chip) * cuts
                at = at + (jnp.bitwise_xor(idx_ref[2], z) if cuts > 1 else 0)
                start = (chip * cuts + z) * rows
                flat_ref[pl.ds(pl.multiple_of(at * rows, 8), rows), :] = ref[start : start + rows, :]


def eliminate(x_ref, vl_ref, vr_ref, r_ref, row_ref, col_ref, base, lo, order, pending):
    hi = lo + BLOCK
    wide = 2 * BLOCK
    rest = order - hi
    row = slice(lo - base, hi - base)
    w = jnp.concatenate(
        leaf(
            [x_ref[lo - base + s : lo - base + s + STRIP, lo:hi] for s in range(0, BLOCK, STRIP)],
            row_ref,
            col_ref,
            pending,
        ),
        axis=0,
    )
    while pending:
        pending.pop(0)()
    if rest:
        v = mm(left3(x_ref[hi - base :, lo:hi]), right3t(w), NT)
        vl_ref[:rest, :] = left3(v)
        vr_ref[:rest, :] = right3t(v)
        near = slice(hi - base, hi - base + BLOCK)
        t = mm(vl_ref[:BLOCK, :], vr_ref[:BLOCK, :], NT)
        x_ref[near, hi : hi + BLOCK] = x_ref[near, hi : hi + BLOCK] - t
    r_ref[:, lo:hi] = right3(w)
    x_ref[row, lo:hi] = w
    if rest:
        x_ref[row, hi:] = jnp.zeros((BLOCK, rest), jnp.float32)

    def update_sums(c, d):
        top = max(c, hi + BLOCK)
        t = mm(vl_ref[top - hi : rest, :], vr_ref[c - hi : d - hi, :], NT)
        x_ref[top - base :, c:d] = x_ref[top - base :, c:d] - t

    def finish_row(c, d):
        t = mm(left3(w), right3(x_ref[row, c:d]))
        x_ref[row, c:d] = t
        r_ref[:, c:d] = right3(t)

    def update_rows(c, d):
        t = mm(vl_ref[:rest, :], r_ref[:, c:d])
        if d <= lo:
            x_ref[hi - base :, c:d] = x_ref[hi - base :, c:d] - t
        else:
            if c < lo:
                x_ref[hi - base :, c:lo] = x_ref[hi - base :, c:lo] - t[:, : lo - c]
            x_ref[hi - base :, lo:hi] = -t[:, lo - c :]

    if rest:
        for c in range(hi, order, wide):
            if max(c, hi + BLOCK) < order:
                pending.append(functools.partial(update_sums, c, min(c + wide, order)))
    for c in range(0, lo, wide):
        pending.append(functools.partial(finish_row, c, min(c + wide, lo)))
    if rest:
        for c in range(0, hi, wide):
            pending.append(functools.partial(update_rows, c, min(c + wide, hi)))


def eliminate_all(x_ref, work, base, first, last, order):
    pending = []
    for lo in range(first, last, BLOCK):
        eliminate(x_ref, *work, base, lo, order, pending)
    for job in pending:
        job()


def head_kernel(parts, head, idx_ref, first_ref, done_ref, rest_ref, mark_ref, x_ref, flat_ref, *work):
    place_bands(first_ref, parts, flat_ref)
    for n, (i, j) in enumerate(lower_blocks(0, head)):
        x_ref[i * BLOCK : (i + 1) * BLOCK, j * BLOCK : (j + 1) * BLOCK] = flat_ref[
            n * BLOCK : (n + 1) * BLOCK, :
        ]
    order = head * BLOCK
    half = order // 2
    eliminate_all(x_ref, work, 0, 0, half, order)
    done_ref[...] = x_ref[:half, :half]
    rest_ref[...] = x_ref[half:, :]
    mark_ref[...] = x_ref[:STRIP, :BLOCK]


def neck_kernel(idx_ref, in_ref, before_ref, x_ref, mark_ref, *work):
    x_ref[...] = in_ref[...]
    half, order = x_ref.shape
    eliminate_all(x_ref, work, half, half, order, order)
    mark_ref[...] = x_ref[:STRIP, :BLOCK]


def tail_kernel(chips, cuts, head, idx_ref, a_ref, b_ref, before_ref, near_ref, far_ref, high_ref, low_ref, *refs):
    parts = 2 * chips
    outs, (x_ref, out_ref, flat_ref), work = refs[:parts], refs[parts : parts + 3], refs[parts + 3 :]
    order = high_ref.shape[0]
    base = head * BLOCK
    place_offsets([near_ref, far_ref], chips, cuts, idx_ref, flat_ref)
    for n, (i, j) in enumerate(lower_blocks(head, order // BLOCK)):
        x_ref[i * BLOCK - base : (i + 1) * BLOCK - base, j * BLOCK : (j + 1) * BLOCK] = flat_ref[
            n * BLOCK : (n + 1) * BLOCK, :
        ]
    half = a_ref.shape[0]
    a, b = halves(a_ref[...]), halves(b_ref[...])
    b_left, b_right = [x[:, :half] for x in b], [x[:, half:] for x in b]
    s_high, s_low = halves(x_ref[:, :base])
    v = mm3(s_high[:, :half], s_low[:, :half], *a, NT)
    v_left = halves(v)
    v = mm3(s_high, s_low, *b, NT)
    v_right = halves(v)
    x_ref[:, :half] = -(mm3(*v_left, *a) + mm3(*v_right, *b_left))
    x_ref[:, half:base] = -mm3(*v_right, *b_right)
    x_ref[:, base:] = x_ref[:, base:] - (mm3(*v_left, *v_left, NT) + mm3(*v_right, *v_right, NT))

    def product(ref, row, first, last):
        x = halves(ref[row : row + last - first, :last])
        out_ref[first:last, :] = mm3(*x, high_ref[:last, :], low_ref[:last, :])

    pending = [
        functools.partial(product, a_ref, 0, 0, half),
        functools.partial(product, b_ref, 0, half, base),
    ]
    for lo in range(base, order, BLOCK):
        eliminate(x_ref, *work, base, lo, order, pending)
        pending.append(functools.partial(product, x_ref, lo - base, lo, lo + BLOCK))
    for job in pending:
        job()
    rows = order // parts
    for d in range(parts):
        at = pl.ds(pl.multiple_of(jnp.bitwise_xor(idx_ref[0], d) * rows, rows), rows)
        outs[d][...] = out_ref[at, :]


def factor_scratch(blocks, rows, order):
    return [
        pltpu.VMEM((len(blocks) * BLOCK, BLOCK), jnp.float32),
        pltpu.VMEM((rows - BLOCK, 3 * BLOCK), jnp.bfloat16),
        pltpu.VMEM((rows - BLOCK, 3 * BLOCK), jnp.bfloat16),
        pltpu.VMEM((3 * BLOCK, order), jnp.bfloat16),
        pltpu.VMEM((BLOCK, BLOCK), jnp.float32),
        pltpu.VMEM((BLOCK * STRIP, BLOCK), jnp.float32),
    ]


def head_factor(first, parts, idx, head):
    rows = head * BLOCK
    half = rows // 2
    return vmem_call(
        functools.partial(head_kernel, parts, head),
        [f32(half, half), f32(half, rows), f32(STRIP, BLOCK)],
        [pltpu.VMEM((rows, rows), jnp.float32)] + factor_scratch(lower_blocks(0, head), rows, rows),
        idx,
        [first],
        cost=3,
    )


def neck_factor(rest, mark, idx):
    half, rows = rest.shape
    return vmem_call(
        neck_kernel,
        [f32(half, rows), f32(STRIP, BLOCK)],
        factor_scratch([], half, rows)[1:],
        idx,
        [rest, mark],
        cost=3,
    )


def tail_product(top, below, mark, second, high, low, chips, cuts, idx, head):
    order, width = high.shape
    rows = order - head * BLOCK
    parts = 2 * chips
    return vmem_call(
        functools.partial(tail_kernel, chips, cuts, head),
        [f32(order // parts, width)] * parts,
        [pltpu.VMEM((rows, order), jnp.float32), pltpu.VMEM((order, width), jnp.float32)]
        + factor_scratch(lower_blocks(head, order // BLOCK), rows, order),
        idx,
        [top, below, mark, *second, high, low],
        cost=25,
        vmem=24,
    )


def local(coeffs):
    band_rows, width = coeffs.shape
    parts = lax.axis_size("band")
    order = band_rows * parts
    columns_all = width * lax.axis_size("ga")
    head = order // BLOCK // 2
    band = lax.axis_index("band")
    idx = jnp.stack([band, band // 2, lax.axis_index("ga")]).astype(jnp.int32)
    pieces = cut_columns(coeffs, band, parts)
    pieces = [pieces[0]] + [swap(pieces[d], "band", d) for d in range(1, parts)]
    keep, send, high, low = gram(pieces, idx, columns_all, head)
    first, second = [sum_chips(p) for p in sum_band(keep, send, head, order, idx)]
    first = sum_first(first)
    second, first = lax.optimization_barrier((sum_second(second, idx), first))
    second = gather_ga(second)
    top, rest, mark = head_factor(first, parts, idx, head)
    second, mark = lax.optimization_barrier((second, mark))
    second = gather_chips(second)
    below, mark = neck_factor(rest, mark, idx)
    second, mark = lax.optimization_barrier((second, mark))
    cuts = lax.axis_size("ga") if lax.axis_size("ga") <= 4 else 1
    result = tail_product(
        top, below, mark, (second, swap(second, "band", 1)), high, low, parts // 2, cuts, idx, head
    )
    result = [result[0]] + [swap(result[d], "band", d) for d in range(1, parts)]
    return join_columns(result, idx)


def solution(mesh):
    return jax.shard_map(
        local,
        mesh=mesh,
        in_specs=(P("band", "ga"),),
        out_specs=P("band", "ga"),
        check_vma=False,
    )
```

```python
import functools

import jax
import jax.numpy as jnp
from jax import lax
from jax.experimental import pallas as pl
from jax.experimental.pallas import tpu as pltpu
from jax.sharding import PartitionSpec as P

BLOCK = 128
STRIP = 8
NN = (((1,), (0,)), ((), ()))
NT = (((1,), (1,)), ((), ()))


def halves(x):
    high = x.astype(jnp.bfloat16)
    return high, (x - high.astype(jnp.float32)).astype(jnp.bfloat16)


def left3(x):
    high, low = halves(x)
    return jnp.concatenate([high, low, high], axis=1)


def right3(x):
    high, low = halves(x)
    return jnp.concatenate([high, high, low], axis=0)


def right3t(x):
    high, low = halves(x)
    return jnp.concatenate([high, high, low], axis=1)


def mm(a, b, dims=NN):
    return lax.dot_general(a, b, dims, preferred_element_type=jnp.float32)


NEAR = 2


def leaf(strips, row_ref, col_ref, pending):
    share = -(-len(pending) // (BLOCK // STRIP - 4))
    strips = list(strips)
    count = len(strips)
    shape = strips[0].shape
    lane = lax.broadcasted_iota(jnp.int32, shape, 1)
    sub = lax.broadcasted_iota(jnp.int32, shape, 0)
    each = range(STRIP)

    def column(x, c):
        return jnp.broadcast_to(x[:, c : c + 1], shape)

    def repeated(ref, r):
        return jnp.broadcast_to(ref[r : r + 1, :], shape)

    for s in range(count):
        base = STRIP * s
        row_ref[base : base + STRIP, :] = strips[s]
        for b in each:
            at = (base + b) * STRIP
            col_ref[at : at + STRIP, :] = column(strips[s], base + b)
        rows = [repeated(row_ref, base + q) for q in each]
        piv = [
            [repeated(col_ref, (base + b) * STRIP + a) if b >= a else None for b in each] for a in each
        ]
        panel = (lane >= base) & (lane < base + STRIP)
        rows = [jnp.where(panel, jnp.where(lane == base + q, 1.0, 0.0), rows[q]) for q in each]
        mult = [[None] * STRIP for _ in each]
        done = [None] * STRIP
        gain = [None] * STRIP
        for q in each:
            root = lax.rsqrt(piv[q][q])
            inv = root * root
            for a in range(q + 1, STRIP):
                mult[a][q] = piv[q][a] * inv
            for a in range(q + 1, STRIP):
                for b in range(a, STRIP):
                    piv[a][b] = piv[a][b] - mult[a][q] * piv[q][b]
                rows[a] = rows[a] - mult[a][q] * rows[q]
            gain[q] = rows[q] * inv
            done[q] = rows[q] * root
        for q in range(STRIP - 1, 0, -1):
            for a in range(q):
                gain[a] = gain[a] - mult[q][a] * gain[q]
        far = s + 1 + NEAR
        for t in range(s + 1, min(far, count)):
            terms = [column(strips[t], base + q) * gain[q] for q in each]
            while len(terms) > 1:
                terms = [terms[i] + terms[i + 1] for i in range(0, len(terms), 2)]
            strips[t] = jnp.where(panel, 0.0, strips[t]) - terms[0]
        if far < count:
            g = gain[0]
            for q in range(1, STRIP):
                g = jnp.where(sub == q, gain[q], g)
            below = STRIP * (count - s - 1)

            def padded(x):
                parts = [x]
                if base:
                    parts = [jnp.zeros((base, BLOCK), x.dtype)] + parts
                if below:
                    parts = parts + [jnp.zeros((below, BLOCK), x.dtype)]
                return jnp.concatenate(parts, axis=0)

            g_high, g_low = [padded(x) for x in halves(g)]
            s_high, s_low = halves(jnp.concatenate(strips[far:], axis=0))
            t = mm(
                jnp.concatenate([s_high, s_low], axis=1), jnp.concatenate([g_high, g_high], axis=0)
            ) + mm(s_high, g_low)
            for i in range(far, count):
                at = STRIP * (i - far)
                strips[i] = jnp.where(panel, 0.0, strips[i]) - t[at : at + STRIP, :]
        new = done[0]
        for q in range(1, STRIP):
            new = jnp.where(sub == q, done[q], new)
        strips[s] = new
        for _ in range(min(share, len(pending))):
            pending.pop(0)()
    return [jnp.where(lane <= sub + STRIP * s, strips[s], 0.0) for s in range(count)]


def vmem_call(kernel, shapes, scratch, idx, operands, cost=1, vmem=12):
    space = pl.BlockSpec(memory_space=pltpu.VMEM)
    return pl.pallas_call(
        kernel,
        out_shape=shapes,
        in_specs=[pl.BlockSpec(memory_space=pltpu.SMEM)] + [space] * len(operands),
        out_specs=[space] * len(shapes),
        scratch_shapes=scratch,
        compiler_params=pltpu.CompilerParams(vmem_limit_bytes=vmem * 2**20),
        cost_estimate=pl.CostEstimate(
            flops=cost * 1_000_000_000, bytes_accessed=0, transcendentals=0
        ),
    )(idx, *operands)


def f32(*shape):
    return jax.ShapeDtypeStruct(shape, jnp.float32)


def cut_columns(x, band, parts):
    width = x.shape[1] // parts
    return [lax.dynamic_slice_in_dim(x, (band ^ d) * width, width, 1) for d in range(parts)]


def join_kernel(parts, width, idx_ref, *refs):
    for d in range(parts):
        start = pl.multiple_of(jnp.bitwise_xor(idx_ref[0], d) * width, width)
        refs[parts][:, pl.ds(start, width)] = refs[d][...]


def join_columns(pieces, idx):
    parts = len(pieces)
    rows, width = pieces[0].shape
    return vmem_call(
        functools.partial(join_kernel, parts, width), [f32(rows, width * parts)], [], idx, pieces, vmem=8
    )[0]


def sum_split_kernel(terms, sections, parts, slot, idx_ref, *refs):
    ins, outs = refs[:terms], list(refs[terms:])
    first = 0
    for length in sections:
        rows = length // parts
        for d in range(parts):
            start = first + jnp.bitwise_xor(idx_ref[slot], d) * rows
            part = pl.ds(pl.multiple_of(start, 8), rows)
            total = ins[0][part, :]
            for r in ins[1:]:
                total = total + r[part, :]
            outs.pop(0)[...] = total
        first += length


def sum_split(terms, sections, parts, slot, idx):
    width = terms[0].shape[1]
    cut = vmem_call(
        functools.partial(sum_split_kernel, len(terms), sections, parts, slot),
        [f32(length // parts, width) for length in sections for _ in range(parts)],
        [],
        idx,
        terms,
    )
    return [cut[n * parts : (n + 1) * parts] for n in range(len(sections))]


def lower_blocks(first, last):
    return [(i, j) for i in range(first, last) for j in range(i + 1)]


def mm3(a_high, a_low, b_high, b_low, dims=NN):
    return mm(a_high, b_high, dims) + mm(a_high, b_low, dims) + mm(a_low, b_high, dims)


def gram_kernel(parts, scale, head, order, idx_ref, *refs):
    pieces = refs[:parts]
    keep_ref, send_ref, high_ref, low_ref, flat_ref = refs[parts:]
    rows = pieces[0].shape[0]
    for d in range(parts):
        at = pl.ds(pl.multiple_of(jnp.bitwise_xor(idx_ref[0], d) * rows, rows), rows)
        high_ref[at, :], low_ref[at, :] = halves(pieces[d][...])
    place = {}
    first = 0
    for blocks in (lower_blocks(0, head), lower_blocks(head, order // BLOCK)):
        half = len(blocks) // 2
        for n, block in enumerate(blocks):
            place[block] = (n // half, first + n % half * BLOCK)
        first += half * BLOCK
    wide = 2 * BLOCK
    for c in range(0, order, wide):
        t = scale * mm3(
            high_ref[c:, :], low_ref[c:, :], high_ref[c : c + wide, :], low_ref[c : c + wide, :], NT
        )
        for i in range(c // BLOCK, order // BLOCK):
            for j in (c // BLOCK, c // BLOCK + 1):
                if j <= i:
                    half, row = place[i, j]
                    flat_ref[half, row : row + BLOCK, :] = t[
                        i * BLOCK - c : (i + 1) * BLOCK - c, j * BLOCK - c : (j + 1) * BLOCK - c
                    ]
    core = jnp.bitwise_and(idx_ref[0], 1)
    keep_ref[...] = flat_ref[core]
    send_ref[...] = flat_ref[1 - core]


def gram(pieces, idx, columns_all, head):
    parts = len(pieces)
    rows, width = pieces[0].shape
    order = rows * parts
    length = len(lower_blocks(0, order // BLOCK)) * BLOCK // 2
    term = jax.ShapeDtypeStruct((order, width), jnp.bfloat16)
    return vmem_call(
        functools.partial(gram_kernel, parts, 1.0 / columns_all, head, order),
        [f32(length, BLOCK), f32(length, BLOCK), term, term],
        [pltpu.VMEM((2, length, BLOCK), jnp.float32)],
        idx,
        pieces,
        vmem=20,
    )


def swap(x, axis, d):
    return lax.ppermute(x, axis, [(i, i ^ d) for i in range(lax.axis_size(axis))])


def sum_all(terms):
    return sum(terms[1:], terms[0])


def sum_band(keep, send, head, order, idx):
    chips = lax.axis_size("band") // 2
    sections = [
        len(blocks) * BLOCK // 2 for blocks in (lower_blocks(0, head), lower_blocks(head, order // BLOCK))
    ]
    return sum_split([keep, swap(send, "band", 1)], sections, chips, 1, idx)


def sum_chips(pieces):
    return [pieces[0]] + [swap(pieces[d], "band", 2 * d) for d in range(1, len(pieces))]


def sum_first(terms):
    depth = lax.axis_size("ga")
    part = sum_all(terms)
    if depth <= 4:
        total = sum_all([part] + [swap(part, "ga", d) for d in range(1, depth)])
    else:
        total = lax.psum(part, "ga")
    return lax.all_gather(total, "band", axis=0, tiled=True)


def sum_second(terms, idx):
    depth = lax.axis_size("ga")
    if depth > 4:
        return lax.psum(sum_all(terms), "ga")
    pieces = sum_split(terms, [terms[0].shape[0]], depth, 2, idx)[0]
    return sum_all([pieces[0]] + [swap(pieces[d], "ga", d) for d in range(1, depth)])


def gather_ga(own):
    depth = lax.axis_size("ga")
    if depth > 4:
        return own
    return jnp.concatenate([own] + [swap(own, "ga", d) for d in range(1, depth)], axis=0)


def gather_chips(own):
    return [own] + [swap(own, "band", 2 * d) for d in range(1, lax.axis_size("band") // 2)]


def place_bands(first_ref, parts, flat_ref):
    rows = first_ref.shape[0] // parts
    for band in range(parts):
        at = ((band % 2) * (parts // 2) + band // 2) * rows
        flat_ref[at : at + rows, :] = first_ref[band * rows : (band + 1) * rows, :]


def place_offsets(halves_, chips, cuts, idx_ref, flat_ref):
    rows = halves_[0].shape[0] // (chips * cuts)
    for c, ref in enumerate(halves_):
        core = jnp.bitwise_xor(jnp.bitwise_and(idx_ref[0], 1), c)
        for chip in range(chips):
            for z in range(cuts):
                at = (core * chips + jnp.bitwise_xor(idx_ref[1], chip)) * cuts
                at = at + (jnp.bitwise_xor(idx_ref[2], z) if cuts > 1 else 0)
                start = (chip * cuts + z) * rows
                flat_ref[pl.ds(pl.multiple_of(at * rows, 8), rows), :] = ref[start : start + rows, :]


def eliminate(x_ref, vl_ref, vr_ref, r_ref, row_ref, col_ref, base, lo, order, pending):
    hi = lo + BLOCK
    wide = 2 * BLOCK
    rest = order - hi
    row = slice(lo - base, hi - base)
    w = jnp.concatenate(
        leaf(
            [x_ref[lo - base + s : lo - base + s + STRIP, lo:hi] for s in range(0, BLOCK, STRIP)],
            row_ref,
            col_ref,
            pending,
        ),
        axis=0,
    )
    while pending:
        pending.pop(0)()
    if rest:
        v = mm(left3(x_ref[hi - base :, lo:hi]), right3t(w), NT)
        vl_ref[:rest, :] = left3(v)
        vr_ref[:rest, :] = right3t(v)
        near = slice(hi - base, hi - base + BLOCK)
        t = mm(vl_ref[:BLOCK, :], vr_ref[:BLOCK, :], NT)
        x_ref[near, hi : hi + BLOCK] = x_ref[near, hi : hi + BLOCK] - t
    r_ref[:, lo:hi] = right3(w)
    x_ref[row, lo:hi] = w
    if rest:
        x_ref[row, hi:] = jnp.zeros((BLOCK, rest), jnp.float32)

    def update_sums(c, d):
        top = max(c, hi + BLOCK)
        t = mm(vl_ref[top - hi : rest, :], vr_ref[c - hi : d - hi, :], NT)
        x_ref[top - base :, c:d] = x_ref[top - base :, c:d] - t

    def finish_row(c, d):
        t = mm(left3(w), right3(x_ref[row, c:d]))
        x_ref[row, c:d] = t
        r_ref[:, c:d] = right3(t)

    def update_rows(c, d):
        t = mm(vl_ref[:rest, :], r_ref[:, c:d])
        if d <= lo:
            x_ref[hi - base :, c:d] = x_ref[hi - base :, c:d] - t
        else:
            if c < lo:
                x_ref[hi - base :, c:lo] = x_ref[hi - base :, c:lo] - t[:, : lo - c]
            x_ref[hi - base :, lo:hi] = -t[:, lo - c :]

    if rest:
        for c in range(hi, order, wide):
            if max(c, hi + BLOCK) < order:
                pending.append(functools.partial(update_sums, c, min(c + wide, order)))
    for c in range(0, lo, wide):
        pending.append(functools.partial(finish_row, c, min(c + wide, lo)))
    if rest:
        for c in range(0, hi, wide):
            pending.append(functools.partial(update_rows, c, min(c + wide, hi)))


def eliminate_all(x_ref, work, base, first, last, order):
    pending = []
    for lo in range(first, last, BLOCK):
        eliminate(x_ref, *work, base, lo, order, pending)
    for job in pending:
        job()


def head_kernel(parts, head, idx_ref, first_ref, done_ref, rest_ref, mark_ref, x_ref, flat_ref, *work):
    place_bands(first_ref, parts, flat_ref)
    for n, (i, j) in enumerate(lower_blocks(0, head)):
        x_ref[i * BLOCK : (i + 1) * BLOCK, j * BLOCK : (j + 1) * BLOCK] = flat_ref[
            n * BLOCK : (n + 1) * BLOCK, :
        ]
    order = head * BLOCK
    half = order // 2
    eliminate_all(x_ref, work, 0, 0, half, order)
    done_ref[...] = x_ref[:half, :half]
    rest_ref[...] = x_ref[half:, :]
    mark_ref[...] = x_ref[:STRIP, :BLOCK]


def neck_kernel(idx_ref, in_ref, before_ref, x_ref, mark_ref, *work):
    x_ref[...] = in_ref[...]
    half, order = x_ref.shape
    eliminate_all(x_ref, work, half, half, order, order)
    mark_ref[...] = x_ref[:STRIP, :BLOCK]


def tail_kernel(chips, cuts, head, idx_ref, a_ref, b_ref, before_ref, near_ref, far_ref, high_ref, low_ref, *refs):
    parts = 2 * chips
    outs, (x_ref, out_ref, flat_ref), work = refs[:parts], refs[parts : parts + 3], refs[parts + 3 :]
    order = high_ref.shape[0]
    base = head * BLOCK
    place_offsets([near_ref, far_ref], chips, cuts, idx_ref, flat_ref)
    for n, (i, j) in enumerate(lower_blocks(head, order // BLOCK)):
        x_ref[i * BLOCK - base : (i + 1) * BLOCK - base, j * BLOCK : (j + 1) * BLOCK] = flat_ref[
            n * BLOCK : (n + 1) * BLOCK, :
        ]
    half = a_ref.shape[0]
    a, b = halves(a_ref[...]), halves(b_ref[...])
    b_left, b_right = [x[:, :half] for x in b], [x[:, half:] for x in b]
    s_high, s_low = halves(x_ref[:, :base])
    v = mm3(s_high[:, :half], s_low[:, :half], *a, NT)
    v_left = halves(v)
    v = mm3(s_high, s_low, *b, NT)
    v_right = halves(v)
    x_ref[:, :half] = -(mm3(*v_left, *a) + mm3(*v_right, *b_left))
    x_ref[:, half:base] = -mm3(*v_right, *b_right)
    x_ref[:, base:] = x_ref[:, base:] - (mm3(*v_left, *v_left, NT) + mm3(*v_right, *v_right, NT))

    def product(ref, row, first, last):
        x = halves(ref[row : row + last - first, :last])
        out_ref[first:last, :] = mm3(*x, high_ref[:last, :], low_ref[:last, :])

    pending = [
        functools.partial(product, a_ref, 0, 0, half),
        functools.partial(product, b_ref, 0, half, base),
    ]
    for lo in range(base, order, BLOCK):
        eliminate(x_ref, *work, base, lo, order, pending)
        pending.append(functools.partial(product, x_ref, lo - base, lo, lo + BLOCK))
    for job in pending:
        job()
    rows = order // parts
    for d in range(parts):
        at = pl.ds(pl.multiple_of(jnp.bitwise_xor(idx_ref[0], d) * rows, rows), rows)
        outs[d][...] = out_ref[at, :]


def factor_scratch(blocks, rows, order):
    return [
        pltpu.VMEM((len(blocks) * BLOCK, BLOCK), jnp.float32),
        pltpu.VMEM((rows - BLOCK, 3 * BLOCK), jnp.bfloat16),
        pltpu.VMEM((rows - BLOCK, 3 * BLOCK), jnp.bfloat16),
        pltpu.VMEM((3 * BLOCK, order), jnp.bfloat16),
        pltpu.VMEM((BLOCK, BLOCK), jnp.float32),
        pltpu.VMEM((BLOCK * STRIP, BLOCK), jnp.float32),
    ]


def head_factor(first, parts, idx, head):
    rows = head * BLOCK
    half = rows // 2
    return vmem_call(
        functools.partial(head_kernel, parts, head),
        [f32(half, half), f32(half, rows), f32(STRIP, BLOCK)],
        [pltpu.VMEM((rows, rows), jnp.float32)] + factor_scratch(lower_blocks(0, head), rows, rows),
        idx,
        [first],
        cost=3,
    )


def neck_factor(rest, mark, idx):
    half, rows = rest.shape
    return vmem_call(
        neck_kernel,
        [f32(half, rows), f32(STRIP, BLOCK)],
        factor_scratch([], half, rows)[1:],
        idx,
        [rest, mark],
        cost=3,
    )


def tail_product(top, below, mark, second, high, low, chips, cuts, idx, head):
    order, width = high.shape
    rows = order - head * BLOCK
    parts = 2 * chips
    return vmem_call(
        functools.partial(tail_kernel, chips, cuts, head),
        [f32(order // parts, width)] * parts,
        [pltpu.VMEM((rows, order), jnp.float32), pltpu.VMEM((order, width), jnp.float32)]
        + factor_scratch(lower_blocks(head, order // BLOCK), rows, order),
        idx,
        [top, below, mark, *second, high, low],
        cost=25,
        vmem=24,
    )


def local(coeffs):
    band_rows, width = coeffs.shape
    parts = lax.axis_size("band")
    order = band_rows * parts
    columns_all = width * lax.axis_size("ga")
    head = order // BLOCK // 2
    band = lax.axis_index("band")
    idx = jnp.stack([band, band // 2, lax.axis_index("ga")]).astype(jnp.int32)
    pieces = cut_columns(coeffs, band, parts)
    pieces = [pieces[0]] + [swap(pieces[d], "band", d) for d in range(1, parts)]
    keep, send, high, low = gram(pieces, idx, columns_all, head)
    first, second = [sum_chips(p) for p in sum_band(keep, send, head, order, idx)]
    first = sum_first(first)
    second, first = lax.optimization_barrier((sum_second(second, idx), first))
    second = gather_ga(second)
    top, rest, mark = head_factor(first, parts, idx, head)
    second, mark = lax.optimization_barrier((second, mark))
    second = gather_chips(second)
    below, mark = neck_factor(rest, mark, idx)
    second, mark = lax.optimization_barrier((second, mark))
    second = jnp.concatenate(second, axis=0)
    cuts = lax.axis_size("ga") if lax.axis_size("ga") <= 4 else 1
    result = tail_product(
        top, below, mark, (second, swap(second, "band", 1)), high, low, parts // 2, cuts, idx, head
    )
    result = [result[0]] + [swap(result[d], "band", d) for d in range(1, parts)]
    return join_columns(result, idx)


def solution(mesh):
    return jax.shard_map(
        local,
        mesh=mesh,
        in_specs=(P("band", "ga"),),
        out_specs=P("band", "ga"),
        check_vma=False,
    )
```

```python
import functools

import jax
import jax.numpy as jnp
from jax import lax
from jax.experimental import pallas as pl
from jax.experimental.pallas import tpu as pltpu
from jax.sharding import PartitionSpec as P

BLOCK = 128
STRIP = 8
NN = (((1,), (0,)), ((), ()))
NT = (((1,), (1,)), ((), ()))


def halves(x):
    high = x.astype(jnp.bfloat16)
    return high, (x - high.astype(jnp.float32)).astype(jnp.bfloat16)


def left3(x):
    high, low = halves(x)
    return jnp.concatenate([high, low, high], axis=1)


def right3(x):
    high, low = halves(x)
    return jnp.concatenate([high, high, low], axis=0)


def right3t(x):
    high, low = halves(x)
    return jnp.concatenate([high, high, low], axis=1)


def mm(a, b, dims=NN):
    return lax.dot_general(a, b, dims, preferred_element_type=jnp.float32)


NEAR = 2


def leaf(strips, row_ref, col_ref, pending):
    share = -(-len(pending) // (BLOCK // STRIP - 4))
    strips = list(strips)
    count = len(strips)
    shape = strips[0].shape
    lane = lax.broadcasted_iota(jnp.int32, shape, 1)
    sub = lax.broadcasted_iota(jnp.int32, shape, 0)
    each = range(STRIP)

    def column(x, c):
        return jnp.broadcast_to(x[:, c : c + 1], shape)

    def repeated(ref, r):
        return jnp.broadcast_to(ref[r : r + 1, :], shape)

    for s in range(count):
        base = STRIP * s
        row_ref[base : base + STRIP, :] = strips[s]
        for b in each:
            at = (base + b) * STRIP
            col_ref[at : at + STRIP, :] = column(strips[s], base + b)
        rows = [repeated(row_ref, base + q) for q in each]
        piv = [
            [repeated(col_ref, (base + b) * STRIP + a) if b >= a else None for b in each] for a in each
        ]
        panel = (lane >= base) & (lane < base + STRIP)
        rows = [jnp.where(panel, jnp.where(lane == base + q, 1.0, 0.0), rows[q]) for q in each]
        mult = [[None] * STRIP for _ in each]
        done = [None] * STRIP
        gain = [None] * STRIP
        for q in each:
            root = lax.rsqrt(piv[q][q])
            inv = root * root
            for a in range(q + 1, STRIP):
                mult[a][q] = piv[q][a] * inv
            for a in range(q + 1, STRIP):
                for b in range(a, STRIP):
                    piv[a][b] = piv[a][b] - mult[a][q] * piv[q][b]
                rows[a] = rows[a] - mult[a][q] * rows[q]
            gain[q] = rows[q] * inv
            done[q] = rows[q] * root
        for q in range(STRIP - 1, 0, -1):
            for a in range(q):
                gain[a] = gain[a] - mult[q][a] * gain[q]
        far = s + 1 + NEAR
        for t in range(s + 1, min(far, count)):
            terms = [column(strips[t], base + q) * gain[q] for q in each]
            while len(terms) > 1:
                terms = [terms[i] + terms[i + 1] for i in range(0, len(terms), 2)]
            strips[t] = jnp.where(panel, 0.0, strips[t]) - terms[0]
        if far < count:
            g = gain[0]
            for q in range(1, STRIP):
                g = jnp.where(sub == q, gain[q], g)
            below = STRIP * (count - s - 1)

            def padded(x):
                parts = [x]
                if base:
                    parts = [jnp.zeros((base, BLOCK), x.dtype)] + parts
                if below:
                    parts = parts + [jnp.zeros((below, BLOCK), x.dtype)]
                return jnp.concatenate(parts, axis=0)

            g_high, g_low = [padded(x) for x in halves(g)]
            s_high, s_low = halves(jnp.concatenate(strips[far:], axis=0))
            t = mm(
                jnp.concatenate([s_high, s_low], axis=1), jnp.concatenate([g_high, g_high], axis=0)
            ) + mm(s_high, g_low)
            for i in range(far, count):
                at = STRIP * (i - far)
                strips[i] = jnp.where(panel, 0.0, strips[i]) - t[at : at + STRIP, :]
        new = done[0]
        for q in range(1, STRIP):
            new = jnp.where(sub == q, done[q], new)
        strips[s] = new
        for _ in range(min(share, len(pending))):
            pending.pop(0)()
    return [jnp.where(lane <= sub + STRIP * s, strips[s], 0.0) for s in range(count)]


def vmem_call(kernel, shapes, scratch, idx, operands, cost=1, vmem=12):
    space = pl.BlockSpec(memory_space=pltpu.VMEM)
    return pl.pallas_call(
        kernel,
        out_shape=shapes,
        in_specs=[pl.BlockSpec(memory_space=pltpu.SMEM)] + [space] * len(operands),
        out_specs=[space] * len(shapes),
        scratch_shapes=scratch,
        compiler_params=pltpu.CompilerParams(vmem_limit_bytes=vmem * 2**20),
        cost_estimate=pl.CostEstimate(
            flops=cost * 1_000_000_000, bytes_accessed=0, transcendentals=0
        ),
    )(idx, *operands)


def f32(*shape):
    return jax.ShapeDtypeStruct(shape, jnp.float32)


def cut_columns(x, band, parts):
    width = x.shape[1] // parts
    return [lax.dynamic_slice_in_dim(x, (band ^ d) * width, width, 1) for d in range(parts)]


def join_kernel(offsets, width, idx_ref, *refs):
    pieces, out_ref, sems = refs[: len(offsets)], refs[-2], refs[-1]
    copies = []
    for n, d in enumerate(offsets):
        start = pl.multiple_of(jnp.bitwise_xor(idx_ref[0], d) * width, width)
        copies.append(
            pltpu.make_async_copy(pieces[n], out_ref.at[:, pl.ds(start, width)], sems.at[n])
        )
    for copy in copies:
        copy.start()
    for copy in copies:
        copy.wait()


def join_columns(pieces, idx):
    parts = len(pieces)
    rows, width = pieces[0].shape
    out = []
    vmem, anywhere = pl.BlockSpec(memory_space=pltpu.VMEM), pl.BlockSpec(memory_space=pl.ANY)
    for offsets in (range(parts // 2), range(parts // 2, parts)):
        out = [
            pl.pallas_call(
                functools.partial(join_kernel, offsets, width),
                out_shape=f32(rows, width * parts),
                in_specs=[pl.BlockSpec(memory_space=pltpu.SMEM)]
                + [vmem] * len(offsets)
                + [anywhere] * len(out),
                out_specs=anywhere,
                scratch_shapes=[pltpu.SemaphoreType.DMA((len(offsets),))],
                input_output_aliases={1 + len(offsets): 0} if out else {},
                compiler_params=pltpu.CompilerParams(vmem_limit_bytes=8 * 2**20),
            )(idx, *[pieces[d] for d in offsets], *out)
        ]
    return out[0]


def sum_split_kernel(terms, sections, parts, slot, idx_ref, *refs):
    ins, outs = refs[:terms], list(refs[terms:])
    first = 0
    for length in sections:
        rows = length // parts
        for d in range(parts):
            start = first + jnp.bitwise_xor(idx_ref[slot], d) * rows
            part = pl.ds(pl.multiple_of(start, 8), rows)
            total = ins[0][part, :]
            for r in ins[1:]:
                total = total + r[part, :]
            outs.pop(0)[...] = total
        first += length


def sum_split(terms, sections, parts, slot, idx):
    width = terms[0].shape[1]
    cut = vmem_call(
        functools.partial(sum_split_kernel, len(terms), sections, parts, slot),
        [f32(length // parts, width) for length in sections for _ in range(parts)],
        [],
        idx,
        terms,
    )
    return [cut[n * parts : (n + 1) * parts] for n in range(len(sections))]


def lower_blocks(first, last):
    return [(i, j) for i in range(first, last) for j in range(i + 1)]


def mm3(a_high, a_low, b_high, b_low, dims=NN):
    return mm(a_high, b_high, dims) + mm(a_high, b_low, dims) + mm(a_low, b_high, dims)


def gram_kernel(parts, scale, head, order, idx_ref, *refs):
    pieces = refs[:parts]
    keep_ref, send_ref, high_ref, low_ref, flat_ref = refs[parts:]
    rows = pieces[0].shape[0]
    for d in range(parts):
        at = pl.ds(pl.multiple_of(jnp.bitwise_xor(idx_ref[0], d) * rows, rows), rows)
        high_ref[at, :], low_ref[at, :] = halves(pieces[d][...])
    place = {}
    first = 0
    for blocks in (lower_blocks(0, head), lower_blocks(head, order // BLOCK)):
        half = len(blocks) // 2
        for n, block in enumerate(blocks):
            place[block] = (n // half, first + n % half * BLOCK)
        first += half * BLOCK
    wide = 2 * BLOCK
    for c in range(0, order, wide):
        t = scale * mm3(
            high_ref[c:, :], low_ref[c:, :], high_ref[c : c + wide, :], low_ref[c : c + wide, :], NT
        )
        for i in range(c // BLOCK, order // BLOCK):
            for j in (c // BLOCK, c // BLOCK + 1):
                if j <= i:
                    half, row = place[i, j]
                    flat_ref[half, row : row + BLOCK, :] = t[
                        i * BLOCK - c : (i + 1) * BLOCK - c, j * BLOCK - c : (j + 1) * BLOCK - c
                    ]
    core = jnp.bitwise_and(idx_ref[0], 1)
    keep_ref[...] = flat_ref[core]
    send_ref[...] = flat_ref[1 - core]


def gram(pieces, idx, columns_all, head):
    parts = len(pieces)
    rows, width = pieces[0].shape
    order = rows * parts
    length = len(lower_blocks(0, order // BLOCK)) * BLOCK // 2
    term = jax.ShapeDtypeStruct((order, width), jnp.bfloat16)
    return vmem_call(
        functools.partial(gram_kernel, parts, 1.0 / columns_all, head, order),
        [f32(length, BLOCK), f32(length, BLOCK), term, term],
        [pltpu.VMEM((2, length, BLOCK), jnp.float32)],
        idx,
        pieces,
        vmem=20,
    )


def swap(x, axis, d):
    return lax.ppermute(x, axis, [(i, i ^ d) for i in range(lax.axis_size(axis))])


def sum_all(terms):
    return sum(terms[1:], terms[0])


def sum_band(keep, send, head, order, idx):
    chips = lax.axis_size("band") // 2
    sections = [
        len(blocks) * BLOCK // 2 for blocks in (lower_blocks(0, head), lower_blocks(head, order // BLOCK))
    ]
    return sum_split([keep, swap(send, "band", 1)], sections, chips, 1, idx)


def sum_chips(pieces):
    return [pieces[0]] + [swap(pieces[d], "band", 2 * d) for d in range(1, len(pieces))]


def sum_first(terms):
    depth = lax.axis_size("ga")
    part = sum_all(terms)
    if depth <= 4:
        total = sum_all([part] + [swap(part, "ga", d) for d in range(1, depth)])
    else:
        total = lax.psum(part, "ga")
    return lax.all_gather(total, "band", axis=0, tiled=True)


def sum_second(terms, idx):
    depth = lax.axis_size("ga")
    if depth > 4:
        return lax.psum(sum_all(terms), "ga")
    pieces = sum_split(terms, [terms[0].shape[0]], depth, 2, idx)[0]
    return sum_all([pieces[0]] + [swap(pieces[d], "ga", d) for d in range(1, depth)])


def gather_ga(own):
    depth = lax.axis_size("ga")
    if depth > 4:
        return own
    return jnp.concatenate([own] + [swap(own, "ga", d) for d in range(1, depth)], axis=0)


def gather_chips(own):
    return [own] + [swap(own, "band", 2 * d) for d in range(1, lax.axis_size("band") // 2)]


def place_bands(first_ref, parts, flat_ref):
    rows = first_ref.shape[0] // parts
    for band in range(parts):
        at = ((band % 2) * (parts // 2) + band // 2) * rows
        flat_ref[at : at + rows, :] = first_ref[band * rows : (band + 1) * rows, :]


def place_offsets(halves_, chips, cuts, idx_ref, flat_ref):
    rows = halves_[0].shape[0] // (chips * cuts)
    for c, ref in enumerate(halves_):
        core = jnp.bitwise_xor(jnp.bitwise_and(idx_ref[0], 1), c)
        for chip in range(chips):
            for z in range(cuts):
                at = (core * chips + jnp.bitwise_xor(idx_ref[1], chip)) * cuts
                at = at + (jnp.bitwise_xor(idx_ref[2], z) if cuts > 1 else 0)
                start = (chip * cuts + z) * rows
                flat_ref[pl.ds(pl.multiple_of(at * rows, 8), rows), :] = ref[start : start + rows, :]


def eliminate(x_ref, vl_ref, vr_ref, r_ref, row_ref, col_ref, base, lo, order, pending):
    hi = lo + BLOCK
    wide = 2 * BLOCK
    rest = order - hi
    row = slice(lo - base, hi - base)
    w = jnp.concatenate(
        leaf(
            [x_ref[lo - base + s : lo - base + s + STRIP, lo:hi] for s in range(0, BLOCK, STRIP)],
            row_ref,
            col_ref,
            pending,
        ),
        axis=0,
    )
    while pending:
        pending.pop(0)()
    if rest:
        v = mm(left3(x_ref[hi - base :, lo:hi]), right3t(w), NT)
        vl_ref[:rest, :] = left3(v)
        vr_ref[:rest, :] = right3t(v)
        near = slice(hi - base, hi - base + BLOCK)
        t = mm(vl_ref[:BLOCK, :], vr_ref[:BLOCK, :], NT)
        x_ref[near, hi : hi + BLOCK] = x_ref[near, hi : hi + BLOCK] - t
    r_ref[:, lo:hi] = right3(w)
    x_ref[row, lo:hi] = w
    if rest:
        x_ref[row, hi:] = jnp.zeros((BLOCK, rest), jnp.float32)

    def update_sums(c, d):
        top = max(c, hi + BLOCK)
        t = mm(vl_ref[top - hi : rest, :], vr_ref[c - hi : d - hi, :], NT)
        x_ref[top - base :, c:d] = x_ref[top - base :, c:d] - t

    def finish_row(c, d):
        t = mm(left3(w), right3(x_ref[row, c:d]))
        x_ref[row, c:d] = t
        r_ref[:, c:d] = right3(t)

    def update_rows(c, d):
        t = mm(vl_ref[:rest, :], r_ref[:, c:d])
        if d <= lo:
            x_ref[hi - base :, c:d] = x_ref[hi - base :, c:d] - t
        else:
            if c < lo:
                x_ref[hi - base :, c:lo] = x_ref[hi - base :, c:lo] - t[:, : lo - c]
            x_ref[hi - base :, lo:hi] = -t[:, lo - c :]

    if rest:
        for c in range(hi, order, wide):
            if max(c, hi + BLOCK) < order:
                pending.append(functools.partial(update_sums, c, min(c + wide, order)))
    for c in range(0, lo, wide):
        pending.append(functools.partial(finish_row, c, min(c + wide, lo)))
    if rest:
        for c in range(0, hi, wide):
            pending.append(functools.partial(update_rows, c, min(c + wide, hi)))


def eliminate_all(x_ref, work, base, first, last, order):
    pending = []
    for lo in range(first, last, BLOCK):
        eliminate(x_ref, *work, base, lo, order, pending)
    for job in pending:
        job()


def head_kernel(parts, head, idx_ref, first_ref, done_ref, rest_ref, mark_ref, x_ref, flat_ref, *work):
    place_bands(first_ref, parts, flat_ref)
    for n, (i, j) in enumerate(lower_blocks(0, head)):
        x_ref[i * BLOCK : (i + 1) * BLOCK, j * BLOCK : (j + 1) * BLOCK] = flat_ref[
            n * BLOCK : (n + 1) * BLOCK, :
        ]
    order = head * BLOCK
    half = order // 2
    eliminate_all(x_ref, work, 0, 0, half, order)
    done_ref[...] = x_ref[:half, :half]
    rest_ref[...] = x_ref[half:, :]
    mark_ref[...] = x_ref[:STRIP, :BLOCK]


def neck_kernel(idx_ref, in_ref, before_ref, x_ref, mark_ref, *work):
    x_ref[...] = in_ref[...]
    half, order = x_ref.shape
    eliminate_all(x_ref, work, half, half, order, order)
    mark_ref[...] = x_ref[:STRIP, :BLOCK]


def tail_kernel(chips, cuts, head, idx_ref, a_ref, b_ref, before_ref, near_ref, far_ref, high_ref, low_ref, *refs):
    parts = 2 * chips
    outs, (x_ref, out_ref, flat_ref), work = refs[:parts], refs[parts : parts + 3], refs[parts + 3 :]
    order = high_ref.shape[0]
    base = head * BLOCK
    place_offsets([near_ref, far_ref], chips, cuts, idx_ref, flat_ref)
    for n, (i, j) in enumerate(lower_blocks(head, order // BLOCK)):
        x_ref[i * BLOCK - base : (i + 1) * BLOCK - base, j * BLOCK : (j + 1) * BLOCK] = flat_ref[
            n * BLOCK : (n + 1) * BLOCK, :
        ]
    half = a_ref.shape[0]
    a, b = halves(a_ref[...]), halves(b_ref[...])
    b_left, b_right = [x[:, :half] for x in b], [x[:, half:] for x in b]
    s_high, s_low = halves(x_ref[:, :base])
    v = mm3(s_high[:, :half], s_low[:, :half], *a, NT)
    v_left = halves(v)
    v = mm3(s_high, s_low, *b, NT)
    v_right = halves(v)
    x_ref[:, :half] = -(mm3(*v_left, *a) + mm3(*v_right, *b_left))
    x_ref[:, half:base] = -mm3(*v_right, *b_right)
    x_ref[:, base:] = x_ref[:, base:] - (mm3(*v_left, *v_left, NT) + mm3(*v_right, *v_right, NT))

    def product(ref, row, first, last):
        x = halves(ref[row : row + last - first, :last])
        out_ref[first:last, :] = mm3(*x, high_ref[:last, :], low_ref[:last, :])

    pending = [
        functools.partial(product, a_ref, 0, 0, half),
        functools.partial(product, b_ref, 0, half, base),
    ]
    for lo in range(base, order, BLOCK):
        eliminate(x_ref, *work, base, lo, order, pending)
        pending.append(functools.partial(product, x_ref, lo - base, lo, lo + BLOCK))
    for job in pending:
        job()
    rows = order // parts
    for d in range(parts):
        at = pl.ds(pl.multiple_of(jnp.bitwise_xor(idx_ref[0], d) * rows, rows), rows)
        outs[d][...] = out_ref[at, :]


def factor_scratch(blocks, rows, order):
    return [
        pltpu.VMEM((len(blocks) * BLOCK, BLOCK), jnp.float32),
        pltpu.VMEM((rows - BLOCK, 3 * BLOCK), jnp.bfloat16),
        pltpu.VMEM((rows - BLOCK, 3 * BLOCK), jnp.bfloat16),
        pltpu.VMEM((3 * BLOCK, order), jnp.bfloat16),
        pltpu.VMEM((BLOCK, BLOCK), jnp.float32),
        pltpu.VMEM((BLOCK * STRIP, BLOCK), jnp.float32),
    ]


def head_factor(first, parts, idx, head):
    rows = head * BLOCK
    half = rows // 2
    return vmem_call(
        functools.partial(head_kernel, parts, head),
        [f32(half, half), f32(half, rows), f32(STRIP, BLOCK)],
        [pltpu.VMEM((rows, rows), jnp.float32)] + factor_scratch(lower_blocks(0, head), rows, rows),
        idx,
        [first],
        cost=3,
    )


def neck_factor(rest, mark, idx):
    half, rows = rest.shape
    return vmem_call(
        neck_kernel,
        [f32(half, rows), f32(STRIP, BLOCK)],
        factor_scratch([], half, rows)[1:],
        idx,
        [rest, mark],
        cost=3,
    )


def tail_product(top, below, mark, second, high, low, chips, cuts, idx, head):
    order, width = high.shape
    rows = order - head * BLOCK
    parts = 2 * chips
    return vmem_call(
        functools.partial(tail_kernel, chips, cuts, head),
        [f32(order // parts, width)] * parts,
        [pltpu.VMEM((rows, order), jnp.float32), pltpu.VMEM((order, width), jnp.float32)]
        + factor_scratch(lower_blocks(head, order // BLOCK), rows, order),
        idx,
        [top, below, mark, *second, high, low],
        cost=25,
        vmem=24,
    )


def local(coeffs):
    band_rows, width = coeffs.shape
    parts = lax.axis_size("band")
    order = band_rows * parts
    columns_all = width * lax.axis_size("ga")
    head = order // BLOCK // 2
    band = lax.axis_index("band")
    idx = jnp.stack([band, band // 2, lax.axis_index("ga")]).astype(jnp.int32)
    pieces = cut_columns(coeffs, band, parts)
    pieces = [pieces[0]] + [swap(pieces[d], "band", d) for d in range(1, parts)]
    keep, send, high, low = gram(pieces, idx, columns_all, head)
    first, second = [sum_chips(p) for p in sum_band(keep, send, head, order, idx)]
    first = sum_first(first)
    second, first = lax.optimization_barrier((sum_second(second, idx), first))
    second = gather_ga(second)
    top, rest, mark = head_factor(first, parts, idx, head)
    second, mark = lax.optimization_barrier((second, mark))
    second = gather_chips(second)
    below, mark = neck_factor(rest, mark, idx)
    second, mark = lax.optimization_barrier((second, mark))
    second = jnp.concatenate(second, axis=0)
    cuts = lax.axis_size("ga") if lax.axis_size("ga") <= 4 else 1
    result = tail_product(
        top, below, mark, (second, swap(second, "band", 1)), high, low, parts // 2, cuts, idx, head
    )
    result = [result[0]] + [swap(result[d], "band", d) for d in range(1, parts)]
    return join_columns(result, idx)


def solution(mesh):
    return jax.shard_map(
        local,
        mesh=mesh,
        in_specs=(P("band", "ga"),),
        out_specs=P("band", "ga"),
        check_vma=False,
    )
```
